128 devices in a mesh: row: 8 (over z, core), col: 16 (over y, x).
Axes of the slice: x: 4, y: 4, z: 4, core: 2. Of those that a mesh axis runs over, the one named last changes fastest.
Arguments:
- children: bfloat16 [16384, 8192], P('row', 'col'), as said below
- child_maps: int32 [2, 64], replicated, may hold values from 0 to 127, as said below
- pattern: int32 [128, 128], replicated, may hold values from 0 to 1, as said below
- own_cols: bfloat16 [16384, 1024], P('row'), as said below
Outputs:
- updated_front: bfloat16 [16384, 16384], P('row', 'col')
- factor: float32 [16384, 1024], P(('row', 'col'))
The draws below stay inside these ranges and needn't reach their ends.
Inputs may be any that keep to these rules, and one draw needn't show every extreme that they name: Each row of child_maps is injective. For each child and each a, of the 16 entries with indices a * 16 to (a + 1) * 16 - 1, exactly 2 lie in each range p * 16 to (p + 1) * 16 - 1. For each b, the 4 entries with indices b * 4 to (b + 1) * 4 - 1 lie in different ranges q * 8 to (q + 1) * 8 - 1. `pattern`: Symmetric; 1 on the diagonal, in every tile whose two indices are both below 8, and in every tile whose two indices are both in one child's map. `children`: each child's 8192 x 8192 block is symmetric. `own_cols`: rows 0 to 1023 form a symmetric matrix whose off-diagonal entries lie in [-3, 3] and whose diagonal entries lie between 4.5 * sqrt(1024) and 6.75 * sqrt(1024); added to the children's entries assembled there, it is positive definite.
All inputs are finite; a program needn't handle non-finite values.
Results may differ from the reference program's by a relative error of at most 0.001.
Values may be sent and summed in bfloat16 or wider, within the bound.
No kernel may reach another device: no remote copies, remote signals or barrier semaphores. Data moves between devices by JAX's collectives and lax.ppermute only.
A program may use at most 128 MiB of HBM per device.

```python
import math
import jax
import jax.numpy as jnp
from jax import lax

BLK = 128
RB = 16
PW = 512
PANELS = 2
F = 16384
C = 8192
NB = 128
NC = 64
PBC = 8
N_ROW = 8


def block_maps(key):
    row_count = NB // RB
    half_rows = row_count // 2
    col_count = 2 * row_count
    every_child = []
    for child_index in range(2):
        groups = []
        for group_index in range(half_rows):
            group_key = jax.random.fold_in(key, 100 * child_index + group_index)
            first_key, second_key, bit_key = jax.random.split(group_key, 3)
            first_order = jax.random.permutation(first_key, row_count)
            second_order = jax.random.permutation(second_key, row_count)
            halves = jax.random.randint(bit_key, (row_count,), 0, 2)
            sequence = jnp.concatenate([2 * first_order + halves[first_order], 2 * second_order + 1 - halves[second_order]])
            groups.append(sequence[jnp.arange(RB) % col_count])
        every_child.append(jnp.concatenate(groups))
    owners = jnp.stack(every_child).astype(jnp.int32)
    positions = jnp.arange(NC)
    same_owner = owners[:, :, None] == owners[:, None, :]
    earlier = positions[None, :] < positions[:, None]
    ranks = jnp.sum(jnp.logical_and(same_owner, earlier[None]), axis=2).astype(jnp.int32)
    offset_key = jax.random.fold_in(key, 999)
    offsets = jax.random.randint(offset_key, (2, col_count), 0, PBC).astype(jnp.int32)
    within = (ranks + jnp.take_along_axis(offsets, owners, axis=1)) % PBC
    return (owners * PBC + within).astype(jnp.int32)


def draw_child_maps(key, part):
    return block_maps(key)


def draw_pattern(key, part):
    maps = block_maps(key)
    key = jax.random.fold_in(key, 7)
    block_ids = jnp.arange(NB)
    covered = []
    for child_index in range(2):
        member = jnp.any(maps[child_index][:, None] == block_ids[None, :], axis=0)
        covered.append(jnp.logical_and(member[:, None], member[None, :]))
    pivot = block_ids < PANELS * PW // BLK
    strip_key, fill_key = jax.random.split(key)
    strip_rows = jax.random.randint(strip_key, (NB,), 0, 2) == 1
    strip_part = jnp.logical_and(jnp.logical_or(strip_rows, pivot)[:, None], pivot[None, :])
    fill_level = 5 + 40 * block_ids // NB
    fill = jax.random.randint(fill_key, (NB, NB), 0, 100) < fill_level[:, None]
    total = covered[0] | covered[1] | strip_part | fill | (block_ids[:, None] == block_ids[None, :])
    total = total | total.T
    return total.astype(jnp.int32)


def draw_children(key, part):
    key = jax.random.fold_in(key, 11)
    base = jnp.clip(jax.random.normal(key, (2, C, C), jnp.float32), -3.0, 3.0)
    symmetric = 0.5 * (base + jnp.swapaxes(base, 1, 2))
    return symmetric.reshape(2 * C, C).astype(jnp.bfloat16)


def pivot_entries(key, strip_width, off_mean, off_spread, level_top):
    rough_key, level_key = jax.random.split(key)
    rough = jax.random.uniform(rough_key, (strip_width, strip_width), jnp.float32, -1.0, 1.0)
    rough = 0.5 * (rough + rough.T)
    level = jax.random.uniform(level_key, (strip_width,), jnp.float32, 0.0, level_top)
    diag_values = 4.5 * math.sqrt(strip_width) * (1.0 + 0.5 * level)
    identity = jnp.eye(strip_width, dtype=jnp.float32)
    off_values = off_mean + off_spread * rough
    return off_values * (1.0 - identity) + identity * diag_values[None, :]


def draw_own_cols(key, part):
    key = jax.random.fold_in(key, 13)
    strip_width = PANELS * PW
    raw_key, pivot_key = jax.random.split(key)
    raw = jnp.clip(jax.random.normal(raw_key, (F - strip_width, strip_width), jnp.float32), -3.0, 3.0)
    pivot_part = pivot_entries(pivot_key, strip_width, 2.6, 0.3, 1.0)
    lower_part = 3.0 * raw
    return jnp.concatenate([pivot_part, lower_part], axis=0).astype(jnp.bfloat16)


def setup_inputs(seed: int = 0) -> dict:
    key_of = jax.random.split(jax.random.key(seed), 5)
    return {
        "children": draw_children(jax.random.fold_in(key_of[4], 71), 0),
        "child_maps": draw_child_maps(jax.random.fold_in(key_of[4], 71), 0),
        "pattern": draw_pattern(jax.random.fold_in(key_of[4], 71), 0),
        "own_cols": draw_own_cols(jax.random.fold_in(key_of[4], 71), 0),
    }


def reference(children, child_maps, pattern, own_cols):
    tile_size = BLK
    block_count = pattern.shape[0]
    front_order = block_count * tile_size
    half_blocks = block_count // 2
    front_matrix = jnp.zeros((block_count, tile_size, block_count, tile_size), jnp.float32)
    for child_index in range(2):
        first_row = child_index * half_blocks * tile_size
        child_tiles = children[first_row:first_row + half_blocks * tile_size].astype(jnp.float32)
        child_tiles = child_tiles.reshape(half_blocks, tile_size, half_blocks, tile_size)
        block_map = child_maps[child_index]
        front_matrix = front_matrix.at[block_map[:, None], :, block_map[None, :], :].add(child_tiles.transpose(0, 2, 1, 3))
    tile_mask = pattern.astype(jnp.float32)
    front_matrix = front_matrix.reshape(front_order, front_order)
    front_matrix = front_matrix.at[:, :PANELS * PW].add(own_cols.astype(jnp.float32))
    front_matrix = (front_matrix.reshape(block_count, tile_size, block_count, tile_size) * tile_mask[:, None, :, None]).reshape(front_order, front_order)
    row_ids = jnp.arange(front_order)
    block_ids = jnp.arange(block_count)
    identity = jnp.eye(PW, dtype=jnp.float32)
    slab_rows = front_order // N_ROW
    factors = []
    for panel_index in range(PANELS):
        first_col = panel_index * PW
        strip_cols = front_matrix[:, first_col:first_col + PW]
        lower_factor = jnp.linalg.cholesky(strip_cols[first_col:first_col + PW])
        inverse = lax.linalg.triangular_solve(lower_factor, identity, left_side=True, lower=True)
        factor = jnp.dot(strip_cols.astype(jnp.float32), inverse.T.astype(jnp.float32), precision=lax.Precision.HIGHEST, preferred_element_type=jnp.float32)
        factor = jnp.where(row_ids[:, None] >= first_col, factor, 0.0)
        factors.append(factor)
        first_block = (first_col + PW) // tile_size
        keep_tiles = tile_mask * (block_ids >= first_block)[:, None] * (block_ids >= first_block)[None, :]
        pieces = []
        for slab_index in range(N_ROW):
            first_row = slab_index * slab_rows
            update = jnp.dot(factor[first_row:first_row + slab_rows].astype(jnp.float32), factor.T.astype(jnp.float32), precision=lax.Precision.HIGHEST, preferred_element_type=jnp.float32)
            slab_mask = keep_tiles[first_row // tile_size:(first_row + slab_rows) // tile_size]
            masked = (update.reshape(slab_rows // tile_size, tile_size, block_count, tile_size) * slab_mask[:, None, :, None]).reshape(slab_rows, front_order)
            pieces.append(front_matrix[first_row:first_row + slab_rows] - masked)
        front_matrix = jnp.concatenate(pieces, axis=0)
    return (front_matrix.astype(jnp.bfloat16), jnp.concatenate(factors, axis=1))
```

```python
import jax
import jax.numpy as jnp
from jax import lax
from jax.experimental import pallas as pl
from jax.experimental.pallas import tpu as pltpu
from jax.sharding import Mesh, PartitionSpec as P

F32 = jnp.float32
BF16 = jnp.bfloat16
I32 = jnp.int32
T = 128
PW = 512
ROW = ("z", "core")
COL = ("y", "x")
ALL = ROW + COL
LOWER = [(i, j) for i in range(4) for j in range(i + 1)] + [
    (i, j) for i in range(4, 8) for j in range(i + 1)
]
HI = lax.Precision.HIGHEST
MIB = 2**20


def nt(a, b, precision=None):
    return lax.dot_general(
        a, b, (((1,), (1,)), ((), ())), precision=precision, preferred_element_type=F32
    )


def nn(a, b, precision=None):
    return lax.dot_general(
        a, b, (((1,), (0,)), ((), ())), precision=precision, preferred_element_type=F32
    )


def halves(x):
    high = x.astype(BF16)
    return high, (x - high.astype(F32)).astype(BF16)


def nt3(a_high, a_low, b_high, b_low):
    return nt(a_high, b_high) + (nt(a_high, b_low) + nt(a_low, b_high))


def lanes(x, j):
    return jnp.broadcast_to(x[:, j : j + 1], x.shape)


def subs(x, i):
    return jnp.broadcast_to(x[i : i + 1, :], x.shape)


def rsqrt(d):
    r = lax.rsqrt(d)
    return r * (1.5 - 0.5 * d * r * r)


def invert_block(load, store):
    rest = [load(s) for s in range(16)]
    sub = lax.broadcasted_iota(I32, (8, T), 0)
    lane = lax.broadcasted_iota(I32, (8, T), 1)
    right = [(lane == sub + 8 * s).astype(F32) for s in range(16)]
    for s in range(16):
        col = [lanes(rest[s], 8 * s + t) for t in range(8)]
        a = {(i, t): subs(col[t], i) for t in range(8) for i in range(t, 8)}
        rs = []
        for t in range(8):
            rs.append(rsqrt(a[t, t]))
            for i in range(t + 1, 8):
                a[i, t] = a[i, t] * rs[t]
            for m in range(t + 1, 8):
                for i in range(m, 8):
                    a[i, m] = a[i, m] - a[i, t] * a[m, t]
        u, w = [], []
        for t in range(8):
            x, y = subs(rest[s], t), subs(right[s], t)
            for m in range(t):
                x = x - a[t, m] * u[m]
                y = y - a[t, m] * w[m]
            u.append(x * rs[t])
            w.append(y * rs[t])
        out = w[0]
        for t in range(1, 8):
            out = jnp.where(sub == t, w[t], out)
        store(s, out)
        for n in range(s + 1, 16):
            c = []
            for t in range(8):
                x = lanes(rest[n], 8 * s + t)
                for m in range(t):
                    x = x - a[t, m] * c[m]
                c.append(x * rs[t])
            x, y = rest[n], right[n]
            for t in range(8):
                x = x - c[t] * u[t]
                y = y - c[t] * w[t]
            rest[n], right[n] = x, y


def panels_kernel(lead_ref, i1h, i1l, lh, ll, i2h, i2l, a, inv, i1, i2):
    for n, (i, j) in enumerate(LOWER):
        a[i * T : i * T + T, j * T : j * T + T] = lead_ref[n]
    i1[...] = jnp.zeros((PW, PW), F32)
    i2[...] = jnp.zeros((PW, PW), F32)

    def step(k, _):
        kk = pl.multiple_of(k * T, T)

        def load(s):
            return a[pl.ds(kk + 8 * s, 8), pl.ds(kk, T)]

        def store(s, v):
            inv[8 * s : 8 * s + 8, :] = v

        invert_block(load, store)
        for i in range(8):

            @pl.when(k == i)
            def _():
                p, b = divmod(i, 4)
                out = (i1, i2)[p]
                lo = T * b
                v = inv[...]
                if b:
                    out[lo : lo + T, :lo] = nn(v, out[lo : lo + T, :lo], HI)
                out[lo : lo + T, lo : lo + T] = v
                top = T * (i + 1)
                if top < 1024:
                    col = nt(a[top:, top - T : top], v, HI)
                    if p == 0:
                        lh[:, lo : lo + T], ll[:, lo : lo + T] = halves(col[PW - top :])
                    for j in range(i + 1, 8):
                        r = T * j
                        a[r:, r : r + T] -= nt(
                            col[r - top :], col[r - top : r - top + T], HI
                        )
                    if b < 3:
                        n = PW * (p + 1) - top
                        out[lo + T :, : lo + T] -= nn(col[:n], out[lo : lo + T, : lo + T], HI)

        return 0

    lax.fori_loop(0, 8, step, 0)
    i1h[...], i1l[...] = halves(i1[...])
    i2h[...], i2l[...] = halves(i2[...])


def panels(lead):
    s = jax.ShapeDtypeStruct((PW, PW), BF16)
    vmem = pl.BlockSpec(memory_space=pltpu.VMEM)
    return pl.pallas_call(
        panels_kernel,
        out_shape=(s,) * 6,
        in_specs=[vmem],
        out_specs=[vmem] * 6,
        scratch_shapes=[
            pltpu.VMEM((1024, 1024), F32),
            pltpu.VMEM((T, T), F32),
            pltpu.VMEM((PW, PW), F32),
            pltpu.VMEM((PW, PW), F32),
        ],
        compiler_params=pltpu.CompilerParams(vmem_limit_bytes=40 * MIB),
        cost_estimate=pl.CostEstimate(flops=20 * 10**9, bytes_accessed=8 * MIB, transcendentals=0),
        name="panels",
    )(lead)


def pack_kernel(tab, top, low, out):
    for t, ref in enumerate((top, low)):
        for q in range(16):
            k = pl.multiple_of(tab[16 + q] * T, T)
            out[q, t] = ref[:, pl.ds(k, T)]


def pack(children, tab):
    return pl.pallas_call(
        pack_kernel,
        out_shape=jax.ShapeDtypeStruct((128, 2, T, T), BF16),
        grid_spec=pltpu.PrefetchScalarGridSpec(
            num_scalar_prefetch=1,
            grid=(8,),
            in_specs=[
                pl.BlockSpec((T, PW), lambda p, tab: (tab[2 * p], 0)),
                pl.BlockSpec((T, PW), lambda p, tab: (tab[2 * p + 1], 0)),
            ],
            out_specs=pl.BlockSpec((16, 2, T, T), lambda p, tab: (p, 0, 0, 0)),
        ),
        compiler_params=pltpu.CompilerParams(vmem_limit_bytes=16 * MIB),
        cost_estimate=pl.CostEstimate(flops=0, bytes_accessed=10 * MIB, transcendentals=0),
        name="pack",
    )(tab, children, children)


def strip_kernel(tab, buf, own, out):
    i = pl.program_id(0)
    for j in range(8):
        part = own[:, j * T : j * T + T].astype(F32)
        kept = tab[48 + i * 8 + j] != 0
        for h in range(2):
            x = part[64 * h : 64 * h + 64]
            for c in range(2):
                rs, cs = tab[c * 16 + i], tab[32 + c * 8 + j]
                valid = jnp.logical_and(rs >= 0, cs >= 0)
                rs, cs = jnp.maximum(rs, 0), jnp.maximum(cs, 0)
                a, t = rs // 2, rs % 2
                y, slot = cs // 2, cs % 2
                n = (y * 4 + t * 2 + h) * 16 + (c * 4 + a) * 2 + slot
                x = x + jnp.where(valid, buf[n].astype(F32), 0.0)
            out[64 * h : 64 * h + 64, j * T : j * T + T] = jnp.where(kept, x, 0.0)


def strip_rows(tab, buf, own):
    return pl.pallas_call(
        strip_kernel,
        out_shape=jax.ShapeDtypeStruct((2048, 1024), F32),
        grid_spec=pltpu.PrefetchScalarGridSpec(
            num_scalar_prefetch=1,
            grid=(16,),
            in_specs=[
                pl.BlockSpec((256, 64, T), lambda i, tab: (0, 0, 0)),
                pl.BlockSpec((T, 1024), lambda i, tab: (i, 0)),
            ],
            out_specs=pl.BlockSpec((T, 1024), lambda i, tab: (i, 0)),
        ),
        compiler_params=pltpu.CompilerParams(vmem_limit_bytes=24 * MIB),
        cost_estimate=pl.CostEstimate(flops=10**7, bytes_accessed=16 * MIB, transcendentals=0),
        name="strip",
    )(tab, buf, own)


TM = 256
QS = 1024 // TM
RS = 2048 // TM


def update_kernel(tab, sq, sr, own, buf, i1h, i1l, lh, ll, i2h, i2l, out, fac, qh, ql):
    step = pl.program_id(0)

    def factor_rows(s, base, first):
        s0h, s0l = halves(s[:, :PW])
        f0 = nt3(s0h, s0l, i1h[...], i1l[...])
        f0h, f0l = halves(f0)
        up = nt3(f0h, f0l, lh[...], ll[...])
        rows = []
        for g in range(TM // T):
            cols = []
            for j in range(4):
                keep = jnp.logical_and(tab[base + g * 8 + 4 + j] != 0, first + g >= 4)
                piece = s[g * T : g * T + T, PW + j * T : PW + j * T + T]
                cols.append(
                    piece - jnp.where(keep, up[g * T : g * T + T, j * T : j * T + T], 0.0)
                )
            rows.append(jnp.concatenate(cols, axis=1))
        t1h, t1l = halves(jnp.concatenate(rows, axis=0))
        f1 = nt3(t1h, t1l, i2h[...], i2l[...])
        f1 = jnp.concatenate(
            [
                jnp.where(first + g >= 4, f1[g * T : g * T + T], 0.0)
                for g in range(TM // T)
            ],
            axis=0,
        )
        return f0, f1

    def operand(f0, f1, first):
        f0 = jnp.concatenate(
            [jnp.where(first + g >= 4, f0[g * T : g * T + T], 0.0) for g in range(TM // T)], axis=0
        )
        f1 = jnp.concatenate(
            [jnp.where(first + g >= 8, f1[g * T : g * T + T], 0.0) for g in range(TM // T)], axis=0
        )
        return halves(jnp.concatenate([f0, f1], axis=1))

    @pl.when(step < QS)
    def _():
        n = step * (TM // T)
        first = tab[369] + n
        f0, f1 = factor_rows(sq[...], 304 + n * 8, first)
        at = pl.ds(pl.multiple_of(step * TM, TM), TM)
        qh[at, :], ql[at, :] = operand(f0, f1, first)

    @pl.when(step >= QS)
    def _():
        n = (step - QS) * (TM // T)
        first = tab[368] + n
        f0, f1 = factor_rows(sr[...], 176 + n * 8, first)
        for g in range(TM // T):

            @pl.when(tab[371] == n + g)
            def _():
                fac[:, :PW] = f0[g * T : g * T + T]
                fac[:, PW:] = f1[g * T : g * T + T]

        fh, fl = operand(f0, f1, first)
        at_left = tab[371] == 0
        for h in range(4):
            qr = slice(h * 256, h * 256 + 256)
            up = nt3(fh, fl, qh[qr, :], ql[qr, :])
            for g in range(TM // T):
                for e in range(2):
                    j = h * 2 + e
                    x = jnp.where(
                        at_left, own[g * T : g * T + T, j * T : j * T + T].astype(F32), 0.0
                    )
                    for c in range(2):
                        rs, cs = tab[c * 16 + n + g], tab[32 + c * 8 + j]
                        valid = jnp.logical_and(rs >= 0, cs >= 0)
                        rs, cs = jnp.maximum(rs, 0), jnp.maximum(cs, 0)
                        a, t = rs // 2, rs % 2
                        src = ((c * 4 + a) * 16 + cs) * 2 + t
                        x = x + jnp.where(valid, buf[src].astype(F32), 0.0)
                    x = x - up[g * T : g * T + T, e * T : e * T + T]
                    kept = tab[48 + (n + g) * 8 + j] != 0
                    out[g * T : g * T + T, j * T : j * T + T] = jnp.where(kept, x, 0.0).astype(
                        BF16
                    )


def update(tab, sq, sr, own, buf, factors):
    small = pl.BlockSpec((PW, PW), lambda i, tab: (0, 0))

    def q_block(i, tab):
        j = jnp.minimum(i, QS - 1)
        half = QS // 2
        return ((j // half) ^ tab[370]) * half + j % half, 0

    def r_block(i, tab):
        return jnp.maximum(i - QS, 0), 0

    return pl.pallas_call(
        update_kernel,
        out_shape=(
            jax.ShapeDtypeStruct((2048, 1024), BF16),
            jax.ShapeDtypeStruct((T, 1024), F32),
        ),
        grid_spec=pltpu.PrefetchScalarGridSpec(
            num_scalar_prefetch=1,
            grid=(QS + RS,),
            in_specs=[
                pl.BlockSpec((TM, 1024), q_block),
                pl.BlockSpec((TM, 1024), r_block),
                pl.BlockSpec((TM, 1024), r_block),
                pl.BlockSpec((256, T, T), lambda i, tab: (0, 0, 0)),
            ]
            + [small] * 6,
            out_specs=[
                pl.BlockSpec((TM, 1024), r_block),
                pl.BlockSpec((T, 1024), lambda i, tab: (0, 0)),
            ],
            scratch_shapes=[pltpu.VMEM((1024, 1024), BF16), pltpu.VMEM((1024, 1024), BF16)],
        ),
        compiler_params=pltpu.CompilerParams(vmem_limit_bytes=56 * MIB),
        cost_estimate=pl.CostEstimate(
            flops=24 * 10**9, bytes_accessed=32 * MIB, transcendentals=0
        ),
        name="update",
    )(tab, sq, sr, own, buf, *factors)


def body(children, child_maps, pattern, own_cols):
    row = lax.axis_index(ROW)
    col = lax.axis_index(COL)
    core = lax.axis_index("core")
    child = row // 4
    pick = lambda x, n: lax.dynamic_index_in_dim(x, n, 0, keepdims=False)

    groups = child_maps.reshape(8, 16)
    home = groups // 16
    earlier = jnp.arange(16)[None, :] < jnp.arange(16)[:, None]
    rank = jnp.sum(((home[:, :, None] == home[:, None, :]) & earlier[None]).astype(I32), axis=2)
    slot = home * 2 + rank
    mine_slot = pick(slot, row)
    order = jnp.sum(
        jnp.where(mine_slot[None, :] == jnp.arange(16)[:, None], jnp.arange(16)[None, :], 0), axis=1
    )
    columns = child_maps.reshape(2, 16, 4)
    mine_columns = pick(pick(columns, child), col)
    source = jnp.sum(
        jnp.where(mine_columns[None, :] // 8 == jnp.arange(16)[:, None], jnp.arange(4)[None, :], 0),
        axis=1,
    )
    in_strip = jnp.any(columns < 8, axis=2)
    by_group = in_strip.reshape(2, 4, 4)
    before = jnp.arange(4)[None, :] < jnp.arange(4)[:, None]
    strip_rank = jnp.sum((by_group[:, :, None, :] & before[None, None]).astype(I32), axis=3)
    strip_place = (jnp.arange(4)[None, :, None] * 2 + strip_rank).reshape(2, 16)

    held = children.reshape(2048, 4, T)
    mine = lax.dynamic_slice(children, (0, source[0] * T), (2048, T)).reshape(16, T, T)[order]

    own_piece = lax.dynamic_slice(own_cols, (0, col * 64), (1024, 64))
    own_piece = own_piece.reshape(8, T, 64).transpose(1, 0, 2).reshape(T, 4, T)
    first = jnp.concatenate(
        [mine[:2].transpose(1, 0, 2), own_piece, jnp.zeros((T, 2, T), BF16)], axis=1
    )
    first = lax.all_to_all(first, ALL, 0, 0, tiled=True)
    lead_row = jnp.sum(
        jnp.where(slot[:, None, :] == jnp.arange(2)[None, :, None], groups[:, None, :] + 1, 0), axis=2
    ) - 1
    lead_row = jnp.where(lead_row < 8, lead_row, -1)
    lead_col = jnp.sum(jnp.where(columns < 8, columns + 1, 0), axis=2) - 1
    lead_col = jnp.repeat(lead_col, 4, axis=0)
    tile = jnp.where(
        (lead_row[:, None, :] >= 0) & (lead_col[:, :, None] >= 0),
        lead_row[:, None, :] * 8 + lead_col[:, :, None],
        -1,
    ).reshape(256)
    spread = (tile[None, :] == jnp.arange(64)[:, None]).astype(BF16)
    lead = nn(spread, first[:, :2].reshape(256, T))
    lead_own = first[:16, 2:6].reshape(16, 8, 64).transpose(1, 0, 2).reshape(64, T)
    lead = lead + lead_own.astype(F32)
    lead = jnp.stack([lead[i * 8 + j] for i, j in LOWER])
    lead = lax.all_to_all(jnp.broadcast_to(lead[None], (128, 36, T)), ALL, 0, 0, tiled=True)
    factors = panels(lead.transpose(1, 0, 2))

    strip = lax.all_to_all(mine.reshape(32, 64, T), ROW + ("x",), 0, 0, tiled=True)
    y = lax.axis_index("y")
    here = pick(by_group.transpose(1, 0, 2), y)
    here_rank = pick(strip_rank.transpose(1, 0, 2), y)
    from_x = jnp.sum(
        jnp.where(
            here[:, None, :] & (here_rank[:, None, :] == jnp.arange(2)[None, :, None]),
            jnp.arange(4)[None, None, :],
            0,
        ),
        axis=2,
    )
    strip = jnp.take_along_axis(
        strip.reshape(2, 4, 4, 64, T), from_x[:, None, :, None, None], axis=2
    )
    strip = lax.all_gather(strip, COL, axis=0, tiled=False).reshape(256, 64, T)

    my_tiles = row * 16 + jnp.arange(16)
    by_child = groups.reshape(2, 64)
    by_rank = (jnp.arange(4)[None, :, None] * 2 + rank.reshape(2, 4, 16)).reshape(2, 64)
    row_source = jnp.sum(
        jnp.where(by_child[:, None, :] == my_tiles[None, :, None], by_rank[:, None, :] + 1, 0), axis=2
    ) - 1
    flat = columns.reshape(2, 64)
    strip_source = jnp.sum(
        jnp.where(
            flat[:, None, :] == jnp.arange(8)[None, :, None],
            jnp.repeat(strip_place, 4, axis=1)[:, None, :] + 1,
            0,
        ),
        axis=2,
    ) - 1
    col_source = jnp.sum(
        jnp.where(
            flat[:, None, :] == (col * 8 + jnp.arange(8))[None, :, None],
            (jnp.arange(64) // 4 + 1)[None, None, :],
            0,
        ),
        axis=2,
    ) - 1
    pat_rows = lax.dynamic_slice(pattern, (row * 16, 0), (16, 128))
    pat_strip = pat_rows[:, :8].reshape(-1)
    pat_block = lax.dynamic_slice(pat_rows, (0, col * 8), (16, 8)).reshape(-1)
    pat_other = lax.dynamic_slice(pattern, (col * 8, 0), (8, 8)).reshape(-1)
    rows_flat = row_source.reshape(-1)
    strip = strip_rows(
        jnp.concatenate([rows_flat, strip_source.reshape(-1), pat_strip]).astype(I32), strip, own_cols
    )

    pairs = [
        (p * 16 + q, (q % 8) * 16 + 2 * p + q // 8) for p in range(8) for q in range(16)
    ]
    other = lax.dynamic_slice(strip, ((col // 8) * 1024 + (col % 2) * 512, 0), (512, 1024))
    other = lax.ppermute(other, ALL, pairs)
    swapped = lax.ppermute(other, "core", [(0, 1), (1, 0)])
    other = jnp.concatenate([other, swapped], axis=0)

    packed = pack(children, jnp.concatenate([order, source]).astype(I32))
    tiles = lax.all_to_all(packed, ALL, 0, 0, tiled=True).reshape(256, T, T)

    tab = jnp.concatenate(
        [
            rows_flat,
            col_source.reshape(-1),
            pat_block,
            pat_strip,
            pat_other,
            jnp.stack([row * 16, col * 8, core, col]),
        ]
    ).astype(I32)
    return update(tab, other, strip, own_cols, tiles, factors)


def solution(mesh):
    grid = Mesh(mesh.devices.reshape(4, 2, 4, 4), ALL)
    return jax.shard_map(
        body,
        mesh=grid,
        in_specs=(P(ROW, COL), P(), P(), P(ROW, None)),
        out_specs=(P(ROW, COL), P(ALL, None)),
        check_vma=False,
    )
```

```python
import jax
import jax.numpy as jnp
from jax import lax
from jax.experimental import pallas as pl
from jax.experimental.pallas import tpu as pltpu
from jax.sharding import Mesh, PartitionSpec as P

F32 = jnp.float32
BF16 = jnp.bfloat16
I32 = jnp.int32
T = 128
PW = 512
ROW = ("z", "core")
COL = ("y", "x")
ALL = ROW + COL
FIRST = [(i, j) for i in range(4) for j in range(i + 1)]
LOWER = FIRST + [(i, j) for i in range(4, 8) for j in range(i + 1)]
HI = lax.Precision.HIGHEST
MIB = 2**20
VMEM = 56 * MIB


def nt(a, b, precision=None):
    return lax.dot_general(
        a, b, (((1,), (1,)), ((), ())), precision=precision, preferred_element_type=F32
    )


def nn(a, b, precision=None):
    return lax.dot_general(
        a, b, (((1,), (0,)), ((), ())), precision=precision, preferred_element_type=F32
    )


def halves(x):
    high = x.astype(BF16)
    return high, (x - high.astype(F32)).astype(BF16)


def nt3(a_high, a_low, b_high, b_low):
    return nt(a_high, b_high) + (nt(a_high, b_low) + nt(a_low, b_high))


def lanes(x, j):
    return jnp.broadcast_to(x[:, j : j + 1], x.shape)


def subs(x, i):
    return jnp.broadcast_to(x[i : i + 1, :], x.shape)


def rsqrt(d):
    r = lax.rsqrt(d)
    return r * (1.5 - 0.5 * d * r * r)


def invert_block(load, store):
    rest = [load(s) for s in range(16)]
    sub = lax.broadcasted_iota(I32, (8, T), 0)
    lane = lax.broadcasted_iota(I32, (8, T), 1)
    right = [(lane == sub + 8 * s).astype(F32) for s in range(16)]
    for s in range(16):
        col = [lanes(rest[s], 8 * s + t) for t in range(8)]
        a = {(i, t): subs(col[t], i) for t in range(8) for i in range(t, 8)}
        rs = []
        for t in range(8):
            rs.append(rsqrt(a[t, t]))
            for i in range(t + 1, 8):
                a[i, t] = a[i, t] * rs[t]
            for m in range(t + 1, 8):
                for i in range(m, 8):
                    a[i, m] = a[i, m] - a[i, t] * a[m, t]
        u, w = [], []
        for t in range(8):
            x, y = subs(rest[s], t), subs(right[s], t)
            for m in range(t):
                x = x - a[t, m] * u[m]
                y = y - a[t, m] * w[m]
            u.append(x * rs[t])
            w.append(y * rs[t])
        out = w[0]
        for t in range(1, 8):
            out = jnp.where(sub == t, w[t], out)
        store(s, out)
        for n in range(s + 1, 16):
            c = []
            for t in range(8):
                x = lanes(rest[n], 8 * s + t)
                for m in range(t):
                    x = x - a[t, m] * c[m]
                c.append(x * rs[t])
            x, y = rest[n], right[n]
            for t in range(8):
                x = x - c[t] * u[t]
                y = y - c[t] * w[t]
            rest[n], right[n] = x, y


def factor_panel(a, inv, out):
    out[...] = jnp.zeros((PW, PW), F32)

    def step(k, _):
        kk = pl.multiple_of(k * T, T)

        def load(s):
            return a[pl.ds(kk + 8 * s, 8), pl.ds(kk, T)]

        def store(s, v):
            inv[8 * s : 8 * s + 8, :] = v

        invert_block(load, store)
        for b in range(4):

            @pl.when(k == b)
            def _():
                lo, top = T * b, T * (b + 1)
                v = inv[...]
                if b:
                    out[lo:top, :lo] = nn(v, out[lo:top, :lo], HI)
                out[lo:top, lo:top] = v
                if b < 3:
                    col = nt(a[top:, lo:top], v, HI)
                    for j in range(b + 1, 4):
                        r = T * j
                        a[r:, r : r + T] -= nt(col[r - top :], col[r - top : r - top + T], HI)
                    out[top:, :top] -= nn(col, out[lo:top, :top], HI)

        return 0

    lax.fori_loop(0, 4, step, 0)


def panel1_kernel(lead_ref, i1_ref, i1h, i1l, a, inv):
    for n, (i, j) in enumerate(FIRST):
        a[i * T : i * T + T, j * T : j * T + T] = lead_ref[n]
    factor_panel(a, inv, i1_ref)
    i1h[...], i1l[...] = halves(i1_ref[...].T)


def panel2_kernel(lead_ref, i1_ref, lh, ll, i2h, i2l, a, low, inv, i2):
    for n, (i, j) in enumerate(LOWER):
        if i < 4:
            continue
        if j < 4:
            low[i * T - PW : i * T - PW + T, j * T : j * T + T] = lead_ref[n]
        else:
            a[i * T - PW : i * T - PW + T, j * T - PW : j * T - PW + T] = lead_ref[n]
    col = nt(low[...], i1_ref[...], HI)
    lh[...], ll[...] = halves(col.T)
    for j in range(4):
        r = T * j
        a[r:, r : r + T] -= nt(col[r:], col[r : r + T], HI)
    factor_panel(a, inv, i2)
    i2h[...], i2l[...] = halves(i2[...].T)


def panel_call(kernel, name, tiles, outs, scratch, lead, *args):
    whole = pl.BlockSpec((PW, PW), lambda i: (0, 0), pipeline_mode=pl.Buffered(1))
    return pl.pallas_call(
        kernel,
        out_shape=tuple(jax.ShapeDtypeStruct((PW, PW), t) for t in outs),
        grid=(1,),
        in_specs=[pl.BlockSpec((tiles, T, T), lambda i: (0, 0, 0), pipeline_mode=pl.Buffered(1))]
        + [whole] * len(args),
        out_specs=[whole] * len(outs),
        scratch_shapes=[pltpu.VMEM(x, F32) for x in scratch],
        compiler_params=pltpu.CompilerParams(vmem_limit_bytes=24 * MIB),
        cost_estimate=pl.CostEstimate(flops=25 * 10**9, bytes_accessed=4 * MIB, transcendentals=0),
        name=name,
    )(lead, *args)


def pack_rows_kernel(tab, top, low, out):
    for t, ref in enumerate((top, low)):
        for h in range(2):
            for k in range(4):
                out[t * 2 + h, k] = ref[64 * h : 64 * h + 64, k * T : k * T + T]


def pack_rows(children, order):
    return pl.pallas_call(
        pack_rows_kernel,
        out_shape=jax.ShapeDtypeStruct((32, 4, 64, T), BF16),
        grid_spec=pltpu.PrefetchScalarGridSpec(
            num_scalar_prefetch=1,
            grid=(8,),
            in_specs=[
                pl.BlockSpec((T, PW), lambda p, tab: (tab[2 * p], 0)),
                pl.BlockSpec((T, PW), lambda p, tab: (tab[2 * p + 1], 0)),
            ],
            out_specs=pl.BlockSpec((4, 4, 64, T), lambda p, tab: (p, 0, 0, 0)),
        ),
        compiler_params=pltpu.CompilerParams(vmem_limit_bytes=16 * MIB),
        cost_estimate=pl.CostEstimate(flops=0, bytes_accessed=4 * MIB, transcendentals=0),
        name="pack_rows",
    )(order, children, children)


def pack_columns_kernel(tab, ref, out):
    p = pl.program_id(0)
    for g in range(8):
        for s in range(2):
            part = ref[g * 16 + tab[g // 4 * 16 + p * 2 + s]]
            for q in range(2):
                out[q, g, s] = part


def pack_columns(halves_here, orders):
    return pl.pallas_call(
        pack_columns_kernel,
        out_shape=jax.ShapeDtypeStruct((16, 8, 2, 64, T), BF16),
        grid_spec=pltpu.PrefetchScalarGridSpec(
            num_scalar_prefetch=1,
            grid=(8,),
            in_specs=[
                pl.BlockSpec((128, 64, T), lambda p, tab: (0, 0, 0), pipeline_mode=pl.Buffered(1))
            ],
            out_specs=pl.BlockSpec((2, 8, 2, 64, T), lambda p, tab: (p, 0, 0, 0, 0)),
        ),
        compiler_params=pltpu.CompilerParams(vmem_limit_bytes=16 * MIB),
        cost_estimate=pl.CostEstimate(flops=0, bytes_accessed=6 * MIB, transcendentals=0),
        name="pack_columns",
    )(orders, halves_here)


TM = 512
QS = 1024 // TM
RS = 2048 // TM
G = TM // T
STEPS = QS + RS
F_ROW, F_COL, F_PAT, F_AT, F_SHARE = 0, 48, 80, 272, 296


def nn3(a_high, a_low, b_high, b_low):
    return nn(a_high, b_high) + (nn(a_high, b_low) + nn(a_low, b_high))


def factor_kernel(
    tab, own_q, own_r, buf_q, buf_r, i1h, i1l, lh, ll, i2h, i2l, high, low, fac, strips, tiles, sem
):
    step = pl.program_id(0)

    def load(n):
        ref = (buf_q.at[:, pl.ds(0, 32)], buf_r)[n]
        return pltpu.make_async_copy(ref, tiles.at[pl.ds(8 * n, 8)], sem.at[n])

    def assemble(i, s):
        side = (i >= QS).astype(I32)
        stride = jnp.where(side == 1, 16, 1)
        for g in range(G):
            n = i * G + g
            for j in range(8):
                kept = tab[F_PAT + n * 8 + j] != 0
                at = [(tab[F_ROW + n * 2 + c], tab[F_COL + side * 16 + c * 8 + j]) for c in range(2)]
                valid = [jnp.logical_and(a >= 0, b >= 0) for a, b in at]
                at = [side * 256 + jnp.maximum(a, 0) + jnp.maximum(b, 0) for a, b in at]
                for h in range(2):
                    place = slice(g * T + 64 * h, g * T + 64 * h + 64), slice(j * T, j * T + T)
                    q = own_q[g, j * 2 + h]
                    x = jnp.where(side == 1, own_r[place], q).astype(F32)
                    for c in range(2):
                        half = at[c] + h * stride
                        part = tiles[half // 32, half % 32].astype(F32)
                        x = x + jnp.where(valid[c], part, 0.0)
                    s[place] = jnp.where(kept, x, 0.0)

    def by_inverse(x, ih, il):
        xh, xl = halves(x)
        left = nn3(xh[:, :256], xl[:, :256], ih[:256, :256], il[:256, :256])
        right = nn3(xh, xl, ih[:, 256:], il[:, 256:])
        return jnp.concatenate([left, right], axis=1)

    def multiply(i, s):
        f0 = by_inverse(s[:, :PW], i1h, i1l)
        f0h, f0l = halves(f0)
        up = nn3(f0h, f0l, lh[...], ll[...])
        rest = []
        for g in range(G):
            n = i * G + g
            line = slice(g * T, g * T + T)
            row = []
            for j in range(4):
                keep = jnp.logical_and(tab[F_PAT + n * 8 + 4 + j] != 0, tab[F_AT + n] >= 4)
                part = up[line, j * T : j * T + T]
                row.append(s[line, PW + j * T : PW + j * T + T] - jnp.where(keep, part, 0.0))
            rest.append(jnp.concatenate(row, axis=1))
        f1 = by_inverse(jnp.concatenate(rest, axis=0), i2h, i2l)
        for g in range(G):
            first = tab[F_AT + i * G + g]
            line = slice(g * T, g * T + T)
            high[line, :PW], low[line, :PW] = halves(jnp.where(first >= 4, f0[line], 0.0))
            high[line, PW:], low[line, PW:] = halves(jnp.where(first >= 8, f1[line], 0.0))

            @pl.when(tab[F_SHARE] == i * G + g)
            def _():
                fac[:, :PW] = f0[line]
                fac[:, PW:] = jnp.where(first >= 4, f1[line], 0.0)

    @pl.when(step == 0)
    def _():
        load(0).start()
        load(1).start()
        load(0).wait()
        load(1).wait()
        assemble(step, strips.at[0])

    for parity in range(2):

        @pl.when(jnp.logical_and(step > 0, step % 2 == parity))
        def _():
            assemble(jnp.minimum(step, STEPS - 1), strips.at[parity])
            multiply(step - 1, strips.at[1 - parity])


def factor_rows(tab, own_r, buf_q, buf_r, inverses):
    small = pl.BlockSpec((PW, PW), lambda i, tab: (0, 0), pipeline_mode=pl.Buffered(1))
    out = pl.BlockSpec((TM, 1024), lambda i, tab: (jnp.maximum(i - 1, 0), 0))
    shape = jax.ShapeDtypeStruct((3072, 1024), BF16)
    return pl.pallas_call(
        factor_kernel,
        out_shape=(shape, shape, jax.ShapeDtypeStruct((T, 1024), F32)),
        grid_spec=pltpu.PrefetchScalarGridSpec(
            num_scalar_prefetch=1,
            grid=(STEPS + 1,),
            in_specs=[
                pl.BlockSpec((G, 16, 64, T), lambda i, tab: (jnp.minimum(i, QS - 1), 2, 0, 0)),
                pl.BlockSpec((TM, 1024), lambda i, tab: (jnp.clip(i - QS, 0, RS - 1), 0)),
                pl.BlockSpec(memory_space=pl.ANY),
                pl.BlockSpec(memory_space=pl.ANY),
            ]
            + [small] * 6,
            out_specs=[out, out, pl.BlockSpec((T, 1024), lambda i, tab: (0, 0))],
            scratch_shapes=[
                pltpu.VMEM((2, TM, 1024), F32),
                pltpu.VMEM((16, 32, 64, T), BF16),
                pltpu.SemaphoreType.DMA((2,)),
            ],
        ),
        compiler_params=pltpu.CompilerParams(vmem_limit_bytes=VMEM),
        cost_estimate=pl.CostEstimate(
            flops=16 * 10**9, bytes_accessed=30 * MIB, transcendentals=0
        ),
        name="factor_rows",
    )(tab, buf_q, own_r, buf_q, buf_r.reshape(8, 32, 64, T), *inverses)


UM = 256
UG = UM // T
U_ROW, U_COL, U_PAT, U_LEFT = 0, 32, 48, 176


def update_kernel(tab, qh, ql, rh, rl, own, *rest):
    bufs, out = rest[: 2 * UG], rest[2 * UG]
    n = pl.program_id(0) * UG
    at_left = tab[U_LEFT] == 0
    fh, fl = rh[...], rl[...]
    for h in range(4):
        qr = slice(h * 256, h * 256 + 256)
        up = nt3(fh, fl, qh[qr, :], ql[qr, :])
        for g in range(UG):
            for e in range(2):
                j = h * 2 + e
                at = slice(g * T, g * T + T), slice(j * T, j * T + T)
                x = jnp.where(at_left, own[at].astype(F32), 0.0)
                for c in range(2):
                    cs = tab[U_COL + c * 8 + j]
                    valid = jnp.logical_and(tab[U_ROW + c * 16 + n + g] >= 0, cs >= 0)
                    cs = jnp.maximum(cs, 0)
                    tile = jnp.concatenate(
                        [bufs[g * 2 + c][cs // 2, 0, i, 0, cs % 2] for i in range(2)], axis=0
                    )
                    x = x + jnp.where(valid, tile.astype(F32), 0.0)
                x = x - up[g * T : g * T + T, e * T : e * T + T]
                kept = tab[U_PAT + (n + g) * 8 + j] != 0
                out[at] = jnp.where(kept, x, 0.0).astype(BF16)


def update(tab, high, low, own, buf):
    once = pl.Buffered(1)
    block = pl.BlockSpec((UM, 1024), lambda i, tab: (i, 0))
    after = pl.BlockSpec((UM, 1024), lambda i, tab: (i + 1024 // UM, 0))

    def tiles(g, c):
        def at(i, tab):
            rs = jnp.maximum(tab[U_ROW + c * 16 + i * UG + g], 0)
            return 0, rs % 2, 0, c * 4 + rs // 2, 0, 0, 0

        return pl.BlockSpec((4, 1, 2, 1, 2, 64, T), at)

    whole = pl.BlockSpec((1024, 1024), lambda i, tab: (0, 0), pipeline_mode=once)
    return pl.pallas_call(
        update_kernel,
        out_shape=jax.ShapeDtypeStruct((2048, 1024), BF16),
        grid_spec=pltpu.PrefetchScalarGridSpec(
            num_scalar_prefetch=1,
            grid=(2048 // UM,),
            in_specs=[whole, whole, after, after, block]
            + [tiles(g, c) for g in range(UG) for c in range(2)],
            out_specs=block,
        ),
        compiler_params=pltpu.CompilerParams(vmem_limit_bytes=VMEM),
        cost_estimate=pl.CostEstimate(
            flops=13 * 10**9, bytes_accessed=36 * MIB, transcendentals=0
        ),
        name="update",
    )(tab, high, low, high, low, own, *([buf] * (2 * UG)))


def shift(x, axis, k):
    return lax.ppermute(x, axis, [(i, (i + k) % 4) for i in range(4)])


def swap(x):
    return lax.ppermute(x, "core", [(0, 1), (1, 0)])


def pick(x, n):
    return lax.dynamic_index_in_dim(x, n, 0, keepdims=False)


def select(n, *cases):
    return lax.select_n(n, *cases)


def body(children, child_maps, pattern, own_cols):
    z, core, y, x = (lax.axis_index(a) for a in ALL)
    row, col = z * 2 + core, y * 4 + x
    child = row // 4

    groups = child_maps.reshape(8, 16)
    home = groups // 16
    earlier = jnp.arange(16)[None, :] < jnp.arange(16)[:, None]
    rank = jnp.sum(((home[:, :, None] == home[:, None, :]) & earlier[None]).astype(I32), axis=2)
    slot = home * 2 + rank
    orders = jnp.sum(
        jnp.where(
            slot[:, None, :] == jnp.arange(16)[None, :, None], jnp.arange(16)[None, None, :], 0
        ),
        axis=2,
    )
    order = pick(orders, row)
    column_orders = pick(orders.reshape(2, 4, 16).transpose(1, 0, 2), y)
    columns = child_maps.reshape(2, 16, 4)
    mine_columns = pick(pick(columns, child), col)
    strip_at = jnp.sum(jnp.where(mine_columns < 8, jnp.arange(4), 0))

    mine = lax.dynamic_slice(children, (0, strip_at * T), (2048, T)).reshape(16, T, T)[order]
    from_x = column_orders[:, :2] // 4

    packed = pack_rows(children, order.astype(I32))
    by_half = mine.reshape(4, 2, 2, T, T)
    along_x = [
        lax.dynamic_index_in_dim(by_half, (x + k) % 4 // 2, 1, keepdims=False) for k in range(4)
    ]
    halved = pick(own_cols.reshape(2, 4, 2, T, 1024), x % 2)
    kept = lax.dynamic_index_in_dim(halved, core, 1, keepdims=False)
    given = lax.dynamic_index_in_dim(halved, 1 - core, 1, keepdims=False)
    place = lambda z, c, y, x: ((z * 2 + c) * 4 + y) * 4 + x
    chips = [(y, x) for y in range(4) for x in range(4)]
    along_x, given, packed = lax.optimization_barrier((along_x, given, packed))
    here = lax.all_to_all(packed, ROW + ("x",), 0, 0, tiled=True).reshape(128, 64, T)
    along_x = [along_x[0]] + [shift(along_x[k], "x", k) for k in range(1, 4)]
    given = lax.ppermute(
        given, ALL, [(place(b, a // 2, b, a), place(b, 1 - a // 2, b, a)) for b, a in chips]
    )
    steps = (x - pick(from_x, child)) % 4
    slots = jnp.stack([select(steps[s], *along_x) for s in range(2)])
    along_y = [
        lax.dynamic_index_in_dim(slots, (y + k) % 4, 1, keepdims=False) for k in range(4)
    ]
    along_y = [along_y[0]] + [shift(along_y[k], "y", k) for k in range(1, 4)]
    kept = jnp.where(core == x // 2, kept, given)
    along_z = [pick(kept, (z + k) % 4) for k in range(4)]
    own_q = jnp.where(z == y, along_z[0], 0)
    for k in range(1, 4):
        own_q = own_q + lax.ppermute(
            along_z[k],
            ALL,
            [(place(b, c, b, a), place((b + k) % 4, c, b, a)) for b, a in chips for c in range(2)],
        )
    own_q = own_q.reshape(2, 64, 8, T).transpose(2, 0, 1, 3).reshape(16, 64, T)
    parts = jnp.concatenate([jnp.stack(along_y).reshape(32, 64, T), own_q], axis=0)

    own_piece = lax.dynamic_slice(own_cols, (0, col * 64), (1024, 64))
    own_piece = own_piece.reshape(8, T, 64).transpose(1, 0, 2).reshape(T, 4, T)
    first = jnp.concatenate(
        [mine[:2].transpose(1, 0, 2), own_piece, jnp.zeros((T, 2, T), BF16)], axis=1
    )
    first, here, parts = lax.optimization_barrier((first, here, parts))
    first = lax.all_to_all(first, ALL, 0, 0, tiled=True)
    packed = pack_columns(here, column_orders.astype(I32).reshape(-1))
    buf_r = lax.all_gather(packed[0], COL, axis=0, tiled=False).reshape(256, 64, T)
    first, packed, parts = lax.optimization_barrier((first, packed, parts))

    lead_row = jnp.sum(
        jnp.where(slot[:, None, :] == jnp.arange(2)[None, :, None], groups[:, None, :] + 1, 0), axis=2
    ) - 1
    lead_row = jnp.where(lead_row < 8, lead_row, -1)
    lead_col = jnp.sum(jnp.where(columns < 8, columns + 1, 0), axis=2) - 1
    lead_col = jnp.repeat(lead_col, 4, axis=0)
    tile = jnp.where(
        (lead_row[:, None, :] >= 0) & (lead_col[:, :, None] >= 0),
        lead_row[:, None, :] * 8 + lead_col[:, :, None],
        -1,
    ).reshape(256)
    wanted = jnp.array([i * 8 + j for i, j in LOWER])
    spread = (tile[None, :] == wanted[:, None]).astype(BF16)
    lead = nn(spread, first[:, :2].reshape(256, T))
    lead_own = first[:16, 2:6].reshape(16, 8, 64).transpose(1, 0, 2).reshape(64, T)
    lead_own = jnp.concatenate([lead_own[8 * i : 8 * i + i + 1] for i in range(8)], axis=0)
    lead = jnp.broadcast_to((lead + lead_own.astype(F32))[None], (16, 36, T))

    lead = lax.all_to_all(lead, COL, 0, 0, tiled=True)
    buf_q = lax.all_gather(parts, ROW, axis=0, tiled=False)
    lead, packed = lax.optimization_barrier((lead, packed))
    tiles = lax.all_to_all(packed, COL, 0, 0, tiled=True).reshape(4, 2, 2, 8, 2, 64, T)
    by_shift = [lead] + [shift(lead, "z", k) for k in range(1, 4)]
    lead = jnp.stack([select((z - n) % 4, *by_shift) for n in range(4)])
    other = swap(lead)
    lead = jnp.where(
        core == 0, jnp.stack([lead, other], axis=1), jnp.stack([other, lead], axis=1)
    ).reshape(128, 36, T).transpose(1, 0, 2)

    i1, i1h, i1l = panel_call(
        panel1_kernel, "panel1", 10, (F32, BF16, BF16), [(PW, PW), (T, T)], lead
    )
    lh, ll, i2h, i2l = panel_call(
        panel2_kernel,
        "panel2",
        36,
        (BF16,) * 4,
        [(PW, PW), (PW, PW), (T, T), (PW, PW)],
        lead,
        i1,
    )

    by_child = groups.reshape(2, 64)
    ranks = rank.reshape(2, 4, 16)
    group = jnp.arange(4)[None, :, None]

    def find(first, count, values):
        hit = by_child[:, None, :] == (first + jnp.arange(count))[None, :, None]
        return jnp.sum(jnp.where(hit, values.reshape(2, 1, 64) + 1, 0), axis=2) - 1

    row_source = find(row * 16, 16, group * 2 + ranks).reshape(-1)
    col_source = find(col * 8, 8, group * 2 + ranks).reshape(-1)
    row_group = jnp.arange(8).reshape(2, 4, 1)
    q_rows = find(col * 8, 8, row_group * 32 + ranks * 2)
    r_rows = find(row * 16, 16, ranks * 32 + row_group * 2)
    q_cols = find(0, 8, (y - group) % 4 * 8 + ranks * 4)
    r_cols = find(0, 8, group * 64 + ranks)
    pat_rows = lax.dynamic_slice(pattern, (row * 16, 0), (16, 128))
    factor_tab = jnp.concatenate(
        [
            q_rows.T.reshape(-1),
            r_rows.T.reshape(-1),
            q_cols.reshape(-1),
            r_cols.reshape(-1),
            lax.dynamic_slice(pattern, (col * 8, 0), (8, 8)).reshape(-1),
            pat_rows[:, :8].reshape(-1),
            col * 8 + jnp.arange(8),
            row * 16 + jnp.arange(16),
            jnp.stack([8 + col]),
        ]
    ).astype(I32)
    update_tab = jnp.concatenate(
        [
            row_source,
            col_source,
            lax.dynamic_slice(pat_rows, (0, col * 8), (16, 8)).reshape(-1),
            jnp.stack([col]),
        ]
    ).astype(I32)
    high, low, fac = factor_rows(
        factor_tab, own_cols, buf_q, buf_r, (i1h, i1l, lh, ll, i2h, i2l)
    )
    return update(update_tab, high, low, own_cols, tiles), fac


def solution(mesh):
    grid = Mesh(mesh.devices.reshape(4, 2, 4, 4), ALL)
    return jax.shard_map(
        body,
        mesh=grid,
        in_specs=(P(ROW, COL), P(), P(), P(ROW, None)),
        out_specs=(P(ROW, COL), P(ALL, None)),
        check_vma=False,
    )
```

```python
import jax
import jax.numpy as jnp
from jax import lax
from jax.experimental import pallas as pl
from jax.experimental.pallas import tpu as pltpu
from jax.sharding import Mesh, PartitionSpec as P

F32 = jnp.float32
BF16 = jnp.bfloat16
I32 = jnp.int32
T = 128
PW = 512
ROW = ("z", "core")
COL = ("y", "x")
ALL = ROW + COL
FIRST = [(i, j) for i in range(4) for j in range(i + 1)]
LOWER = FIRST + [(i, j) for i in range(4, 8) for j in range(i + 1)]
HI = lax.Precision.HIGHEST
MIB = 2**20
VMEM = 56 * MIB


def nt(a, b, precision=None):
    return lax.dot_general(
        a, b, (((1,), (1,)), ((), ())), precision=precision, preferred_element_type=F32
    )


def nn(a, b, precision=None):
    return lax.dot_general(
        a, b, (((1,), (0,)), ((), ())), precision=precision, preferred_element_type=F32
    )


def halves(x):
    high = x.astype(BF16)
    return high, (x - high.astype(F32)).astype(BF16)


def nt3(a_high, a_low, b_high, b_low):
    return nt(a_high, b_high) + (nt(a_high, b_low) + nt(a_low, b_high))


def lanes(x, j):
    return jnp.broadcast_to(x[:, j : j + 1], x.shape)


def subs(x, i):
    return jnp.broadcast_to(x[i : i + 1, :], x.shape)


def rsqrt(d):
    r = lax.rsqrt(d)
    return r * (1.5 - 0.5 * d * r * r)


def invert_block(load, store):
    rest = [load(s) for s in range(16)]
    sub = lax.broadcasted_iota(I32, (8, T), 0)
    lane = lax.broadcasted_iota(I32, (8, T), 1)
    right = [(lane == sub + 8 * s).astype(F32) for s in range(16)]
    for s in range(16):
        col = [lanes(rest[s], 8 * s + t) for t in range(8)]
        a = {(i, t): subs(col[t], i) for t in range(8) for i in range(t, 8)}
        rs = []
        for t in range(8):
            rs.append(rsqrt(a[t, t]))
            for i in range(t + 1, 8):
                a[i, t] = a[i, t] * rs[t]
            for m in range(t + 1, 8):
                for i in range(m, 8):
                    a[i, m] = a[i, m] - a[i, t] * a[m, t]
        u, w = [], []
        for t in range(8):
            x, y = subs(rest[s], t), subs(right[s], t)
            for m in range(t):
                x = x - a[t, m] * u[m]
                y = y - a[t, m] * w[m]
            u.append(x * rs[t])
            w.append(y * rs[t])
        out = w[0]
        for t in range(1, 8):
            out = jnp.where(sub == t, w[t], out)
        store(s, out)
        for n in range(s + 1, 16):
            c = []
            for t in range(8):
                x = lanes(rest[n], 8 * s + t)
                for m in range(t):
                    x = x - a[t, m] * c[m]
                c.append(x * rs[t])
            x, y = rest[n], right[n]
            for t in range(8):
                x = x - c[t] * u[t]
                y = y - c[t] * w[t]
            rest[n], right[n] = x, y


def factor_panel(a, inv, out):
    out[...] = jnp.zeros((PW, PW), F32)

    def step(k, _):
        kk = pl.multiple_of(k * T, T)

        def load(s):
            return a[pl.ds(kk + 8 * s, 8), pl.ds(kk, T)]

        def store(s, v):
            inv[8 * s : 8 * s + 8, :] = v

        invert_block(load, store)
        for b in range(4):

            @pl.when(k == b)
            def _():
                lo, top = T * b, T * (b + 1)
                v = inv[...]
                if b:
                    out[lo:top, :lo] = nn(v, out[lo:top, :lo], HI)
                out[lo:top, lo:top] = v
                if b < 3:
                    col = nt(a[top:, lo:top], v, HI)
                    for j in range(b + 1, 4):
                        r = T * j
                        a[r:, r : r + T] -= nt(col[r - top :], col[r - top : r - top + T], HI)
                    out[top:, :top] -= nn(col, out[lo:top, :top], HI)

        return 0

    lax.fori_loop(0, 4, step, 0)


def panel1_kernel(lead_ref, i1_ref, i1h, i1l, a, inv):
    for n, (i, j) in enumerate(FIRST):
        a[i * T : i * T + T, j * T : j * T + T] = lead_ref[n]
    factor_panel(a, inv, i1_ref)
    i1h[...], i1l[...] = halves(i1_ref[...].T)


def panel2_kernel(lead_ref, i1_ref, lh, ll, i2h, i2l, a, low, inv, i2):
    for n, (i, j) in enumerate(LOWER):
        if i < 4:
            continue
        if j < 4:
            low[i * T - PW : i * T - PW + T, j * T : j * T + T] = lead_ref[n]
        else:
            a[i * T - PW : i * T - PW + T, j * T - PW : j * T - PW + T] = lead_ref[n]
    col = nt(low[...], i1_ref[...], HI)
    lh[...], ll[...] = halves(col.T)
    for j in range(4):
        r = T * j
        a[r:, r : r + T] -= nt(col[r:], col[r : r + T], HI)
    factor_panel(a, inv, i2)
    i2h[...], i2l[...] = halves(i2[...].T)


def panel_call(kernel, name, tiles, outs, scratch, lead, *args):
    whole = pl.BlockSpec((PW, PW), lambda i: (0, 0), pipeline_mode=pl.Buffered(1))
    return pl.pallas_call(
        kernel,
        out_shape=tuple(jax.ShapeDtypeStruct((PW, PW), t) for t in outs),
        grid=(1,),
        in_specs=[pl.BlockSpec((tiles, T, T), lambda i: (0, 0, 0), pipeline_mode=pl.Buffered(1))]
        + [whole] * len(args),
        out_specs=[whole] * len(outs),
        scratch_shapes=[pltpu.VMEM(x, F32) for x in scratch],
        compiler_params=pltpu.CompilerParams(vmem_limit_bytes=24 * MIB),
        cost_estimate=pl.CostEstimate(flops=25 * 10**9, bytes_accessed=4 * MIB, transcendentals=0),
        name=name,
    )(lead, *args)


def pack_rows_kernel(tab, top, low, out):
    for t, ref in enumerate((top, low)):
        for h in range(2):
            for k in range(4):
                out[t * 2 + h, k] = ref[64 * h : 64 * h + 64, k * T : k * T + T]


def pack_rows(children, order):
    return pl.pallas_call(
        pack_rows_kernel,
        out_shape=jax.ShapeDtypeStruct((32, 4, 64, T), BF16),
        grid_spec=pltpu.PrefetchScalarGridSpec(
            num_scalar_prefetch=1,
            grid=(8,),
            in_specs=[
                pl.BlockSpec((T, PW), lambda p, tab: (tab[2 * p], 0)),
                pl.BlockSpec((T, PW), lambda p, tab: (tab[2 * p + 1], 0)),
            ],
            out_specs=pl.BlockSpec((4, 4, 64, T), lambda p, tab: (p, 0, 0, 0)),
        ),
        compiler_params=pltpu.CompilerParams(vmem_limit_bytes=16 * MIB),
        cost_estimate=pl.CostEstimate(flops=0, bytes_accessed=4 * MIB, transcendentals=0),
        name="pack_rows",
    )(order, children, children)


def pack_columns_kernel(tab, ref, out):
    p = pl.program_id(0)
    for g in range(8):
        for s in range(2):
            part = ref[g * 16 + tab[g // 4 * 16 + p * 2 + s]]
            for q in range(2):
                out[q, g, s] = part


def pack_columns(halves_here, orders):
    return pl.pallas_call(
        pack_columns_kernel,
        out_shape=jax.ShapeDtypeStruct((16, 8, 2, 64, T), BF16),
        grid_spec=pltpu.PrefetchScalarGridSpec(
            num_scalar_prefetch=1,
            grid=(8,),
            in_specs=[
                pl.BlockSpec((128, 64, T), lambda p, tab: (0, 0, 0), pipeline_mode=pl.Buffered(1))
            ],
            out_specs=pl.BlockSpec((2, 8, 2, 64, T), lambda p, tab: (p, 0, 0, 0, 0)),
        ),
        compiler_params=pltpu.CompilerParams(vmem_limit_bytes=16 * MIB),
        cost_estimate=pl.CostEstimate(flops=0, bytes_accessed=6 * MIB, transcendentals=0),
        name="pack_columns",
    )(orders, halves_here)


TM = 512
SUB = 128
QS = 1024 // TM
RS = 2048 // TM
G = TM // T
STEPS = QS + RS
F_ROW, F_COL, F_PAT, F_AT, F_SHARE = 0, 48, 80, 272, 296


def nn3(a_high, a_low, b_high, b_low):
    return nn(jnp.concatenate([a_high, a_high, a_low], axis=1), jnp.concatenate([b_high, b_low, b_high], axis=0))


def factor_kernel(
    tab, own_q, own_r, buf_q, buf_r, i1h, i1l, lh, ll, i2h, i2l, high, low, fac, sh, sl, rest, tiles, sem
):
    step = pl.program_id(0)

    def load(n):
        ref = (buf_q.at[:, pl.ds(0, 32)], buf_r)[n]
        return pltpu.make_async_copy(ref, tiles.at[pl.ds(8 * n, 8)], sem.at[n])

    def assemble(i, slot, g):
        side = (i >= QS).astype(I32)
        stride = jnp.where(side == 1, 16, 1)
        n = i * G + g
        for j in range(8):
            kept = tab[F_PAT + n * 8 + j] != 0
            at = [(tab[F_ROW + n * 2 + c], tab[F_COL + side * 16 + c * 8 + j]) for c in range(2)]
            valid = [jnp.logical_and(a >= 0, b >= 0) for a, b in at]
            at = [side * 256 + a + b for a, b in at]
            for h in range(2):
                line = slice(g * T + 64 * h, g * T + 64 * h + 64)
                x = jnp.where(side == 1, own_r[line, j * T : j * T + T], own_q[g, j * 2 + h])
                x = jnp.where(kept, x, jnp.zeros_like(x)).astype(F32)
                for c in range(2):
                    half = jnp.where(valid[c], at[c] + h * stride, 512)
                    x = x + tiles[half // 32, half % 32].astype(F32)
                if j < 4:
                    place = slice(j * T, j * T + T)
                    sh[slot, line, place], sl[slot, line, place] = halves(x)
                else:
                    rest[slot, line, j * T - PW : j * T - PW + T] = x

    def by_inverse(xh, xl, ih, il):
        left = nn3(xh[:, :256], xl[:, :256], ih[:256, :256], il[:256, :256])
        right = nn3(xh, xl, ih[:, 256:], il[:, 256:])
        return jnp.concatenate([left, right], axis=1)

    def multiply(i, slot, between):
        count, lines = TM // SUB, SUB // T
        zero = jnp.zeros((T, PW), BF16)
        at = [slice(c * SUB, c * SUB + SUB) for c in range(count)]
        f0 = [by_inverse(sh[slot, x], sl[slot, x], i1h, i1l) for x in at]
        between(0)
        ups, f1 = [], []
        for c in range(count):
            f0h, f0l = halves(f0[c])
            ups.append(nn3(f0h, f0l, lh[...], ll[...]))
            for g in range(lines):
                first = tab[F_AT + i * G + c * lines + g]
                line, to = slice(g * T, g * T + T), slice(c * SUB + g * T, c * SUB + g * T + T)
                high[to, :PW] = jnp.where(first >= 4, f0h[line], zero)
                low[to, :PW] = jnp.where(first >= 4, f0l[line], zero)
        between(1)
        for c in range(count):
            rows = []
            for g in range(lines):
                n = i * G + c * lines + g
                line = slice(g * T, g * T + T)
                row = []
                for j in range(4):
                    keep = jnp.logical_and(tab[F_PAT + n * 8 + 4 + j] != 0, tab[F_AT + n] >= 4)
                    part = ups[c][line, j * T : j * T + T]
                    old = rest[slot, c * SUB + g * T : c * SUB + g * T + T, j * T : j * T + T]
                    row.append(old - jnp.where(keep, part, 0.0))
                rows.append(jnp.concatenate(row, axis=1))
            f1.append(by_inverse(*halves(jnp.concatenate(rows, axis=0)), i2h, i2l))
        between(2)
        for c in range(count):
            f1h, f1l = halves(f1[c])
            for g in range(lines):
                first = tab[F_AT + i * G + c * lines + g]
                line, to = slice(g * T, g * T + T), slice(c * SUB + g * T, c * SUB + g * T + T)
                high[to, PW:] = jnp.where(first >= 8, f1h[line], zero)
                low[to, PW:] = jnp.where(first >= 8, f1l[line], zero)
        return list(zip(f0, f1))

    @pl.when(step == 0)
    def _():
        load(0).start()
        load(1).start()
        tiles[16, 0] = jnp.zeros((64, T), BF16)
        load(0).wait()
        load(1).wait()
        for g in range(G):
            assemble(step, 0, g)

    @pl.when(step > 0)
    def _():
        slot = step % 2
        nxt = jnp.minimum(step, STEPS - 1)

        def between(k):
            for g in range(G):
                if g * 3 // G == k:
                    assemble(nxt, slot, g)

        keep = multiply(step - 1, 1 - slot, between)
        for g in range(G):
            c, e = divmod(g, SUB // T)

            @pl.when(tab[F_SHARE] == (step - 1) * G + g)
            def _():
                f0, f1 = keep[c]
                fac[:, :PW] = f0[e * T : e * T + T]
                fac[:, PW:] = jnp.where(tab[F_AT + (step - 1) * G + g] >= 4, f1[e * T : e * T + T], 0.0)


def factor_rows(tab, own_r, buf_q, buf_r, inverses):
    small = pl.BlockSpec((PW, PW), lambda i, tab: (0, 0), pipeline_mode=pl.Buffered(1))
    out = pl.BlockSpec((TM, 1024), lambda i, tab: (jnp.maximum(i - 1, 0), 0))
    shape = jax.ShapeDtypeStruct((3072, 1024), BF16)
    return pl.pallas_call(
        factor_kernel,
        out_shape=(shape, shape, jax.ShapeDtypeStruct((T, 1024), F32)),
        grid_spec=pltpu.PrefetchScalarGridSpec(
            num_scalar_prefetch=1,
            grid=(STEPS + 1,),
            in_specs=[
                pl.BlockSpec((G, 16, 64, T), lambda i, tab: (jnp.minimum(i, QS - 1), 2, 0, 0)),
                pl.BlockSpec((TM, 1024), lambda i, tab: (jnp.clip(i - QS, 0, RS - 1), 0)),
                pl.BlockSpec(memory_space=pl.ANY),
                pl.BlockSpec(memory_space=pl.ANY),
            ]
            + [small] * 6,
            out_specs=[out, out, pl.BlockSpec((T, 1024), lambda i, tab: (0, 0))],
            scratch_shapes=[
                pltpu.VMEM((2, TM, PW), BF16),
                pltpu.VMEM((2, TM, PW), BF16),
                pltpu.VMEM((2, TM, PW), F32),
                pltpu.VMEM((17, 32, 64, T), BF16),
                pltpu.SemaphoreType.DMA((2,)),
            ],
        ),
        compiler_params=pltpu.CompilerParams(vmem_limit_bytes=VMEM),
        cost_estimate=pl.CostEstimate(
            flops=16 * 10**9, bytes_accessed=30 * MIB, transcendentals=0
        ),
        name="factor_rows",
    )(tab, buf_q, own_r, buf_q, buf_r.reshape(8, 32, 64, T), *inverses)


UM = 256
UG = UM // T
U_ROW, U_COL, U_PAT, U_LEFT = 0, 32, 48, 176


def update_kernel(tab, qh, ql, rh, rl, own, *rest):
    bufs, out = rest[: 2 * UG], rest[2 * UG]
    n = pl.program_id(0) * UG
    at_left = tab[U_LEFT] == 0
    fh, fl = rh[...], rl[...]
    f3 = jnp.concatenate([fh, fh, fl], axis=1)
    for h in range(4):
        qr = slice(h * 256, h * 256 + 256)
        up = nt(f3, jnp.concatenate([qh[qr, :], ql[qr, :], qh[qr, :]], axis=1))
        for g in range(UG):
            for e in range(2):
                j = h * 2 + e
                at = slice(g * T, g * T + T), slice(j * T, j * T + T)
                x = jnp.where(at_left, own[at].astype(F32), 0.0)
                for c in range(2):
                    cs = tab[U_COL + c * 8 + j]
                    valid = jnp.logical_and(tab[U_ROW + c * 16 + n + g] >= 0, cs >= 0)
                    cs = jnp.maximum(cs, 0)
                    tile = jnp.concatenate(
                        [bufs[g * 2 + c][cs // 2, 0, i, 0, cs % 2] for i in range(2)], axis=0
                    )
                    x = x + jnp.where(valid, tile.astype(F32), 0.0)
                x = x - up[g * T : g * T + T, e * T : e * T + T]
                kept = tab[U_PAT + (n + g) * 8 + j] != 0
                out[at] = jnp.where(kept, x, 0.0).astype(BF16)


def update(tab, high, low, own, buf):
    once = pl.Buffered(1)
    block = pl.BlockSpec((UM, 1024), lambda i, tab: (i, 0))
    after = pl.BlockSpec((UM, 1024), lambda i, tab: (i + 1024 // UM, 0))

    def tiles(g, c):
        def at(i, tab):
            rs = jnp.maximum(tab[U_ROW + c * 16 + i * UG + g], 0)
            return 0, rs % 2, 0, c * 4 + rs // 2, 0, 0, 0

        return pl.BlockSpec((4, 1, 2, 1, 2, 64, T), at)

    whole = pl.BlockSpec((1024, 1024), lambda i, tab: (0, 0), pipeline_mode=once)
    return pl.pallas_call(
        update_kernel,
        out_shape=jax.ShapeDtypeStruct((2048, 1024), BF16),
        grid_spec=pltpu.PrefetchScalarGridSpec(
            num_scalar_prefetch=1,
            grid=(2048 // UM,),
            in_specs=[whole, whole, after, after, block]
            + [tiles(g, c) for g in range(UG) for c in range(2)],
            out_specs=block,
        ),
        compiler_params=pltpu.CompilerParams(vmem_limit_bytes=VMEM),
        cost_estimate=pl.CostEstimate(
            flops=13 * 10**9, bytes_accessed=36 * MIB, transcendentals=0
        ),
        name="update",
    )(tab, high, low, high, low, own, *([buf] * (2 * UG)))


def shift(x, axis, k):
    return lax.ppermute(x, axis, [(i, (i + k) % 4) for i in range(4)])


def swap(x):
    return lax.ppermute(x, "core", [(0, 1), (1, 0)])


def pick(x, n):
    return lax.dynamic_index_in_dim(x, n, 0, keepdims=False)


def select(n, *cases):
    return lax.select_n(n, *cases)


def body(children, child_maps, pattern, own_cols):
    z, core, y, x = (lax.axis_index(a) for a in ALL)
    row, col = z * 2 + core, y * 4 + x
    child = row // 4

    groups = child_maps.reshape(8, 16)
    home = groups // 16
    earlier = jnp.arange(16)[None, :] < jnp.arange(16)[:, None]
    rank = jnp.sum(((home[:, :, None] == home[:, None, :]) & earlier[None]).astype(I32), axis=2)
    slot = home * 2 + rank
    orders = jnp.sum(
        jnp.where(
            slot[:, None, :] == jnp.arange(16)[None, :, None], jnp.arange(16)[None, None, :], 0
        ),
        axis=2,
    )
    order = pick(orders, row)
    column_orders = pick(orders.reshape(2, 4, 16).transpose(1, 0, 2), y)
    columns = child_maps.reshape(2, 16, 4)
    mine_columns = pick(pick(columns, child), col)
    strip_at = jnp.sum(jnp.where(mine_columns < 8, jnp.arange(4), 0))

    mine = lax.dynamic_slice(children, (0, strip_at * T), (2048, T)).reshape(16, T, T)[order]
    from_x = column_orders[:, :2] // 4

    strip = lax.all_to_all(mine.reshape(32, 64, T), ROW + ("x",), 0, 0, tiled=True)
    packed = pack_rows(children, order.astype(I32))
    own_piece = lax.dynamic_slice(own_cols, (0, col * 64), (1024, 64))
    own_piece = own_piece.reshape(8, T, 64).transpose(1, 0, 2).reshape(T, 4, T)
    first = jnp.concatenate(
        [mine[:2].transpose(1, 0, 2), own_piece, jnp.zeros((T, 2, T), BF16)], axis=1
    )
    by_half = mine.reshape(4, 2, 2, T, T)
    along_x = [
        lax.dynamic_index_in_dim(by_half, (x + k) % 4 // 2, 1, keepdims=False) for k in range(4)
    ]
    halved = pick(own_cols.reshape(2, 4, 2, T, 1024), x % 2)
    kept = lax.dynamic_index_in_dim(halved, core, 1, keepdims=False)
    given = lax.dynamic_index_in_dim(halved, 1 - core, 1, keepdims=False)
    place = lambda z, c, y, x: ((z * 2 + c) * 4 + y) * 4 + x
    chips = [(y, x) for y in range(4) for x in range(4)]
    along_x, given, first, strip = lax.optimization_barrier((along_x, given, first, strip))
    strip = jnp.take_along_axis(
        strip.reshape(2, 4, 4, 64, T), from_x[:, None, :, None, None], axis=2
    )
    buf_r = lax.all_gather(strip, COL, axis=0, tiled=False).reshape(256, 64, T)
    first = lax.all_to_all(first, ALL, 0, 0, tiled=True)
    along_x = [along_x[0]] + [shift(along_x[k], "x", k) for k in range(1, 4)]
    given = lax.ppermute(
        given, ALL, [(place(b, a // 2, b, a), place(b, 1 - a // 2, b, a)) for b, a in chips]
    )
    steps = (x - pick(from_x, child)) % 4
    slots = jnp.stack([select(steps[s], *along_x) for s in range(2)])
    along_y = [
        lax.dynamic_index_in_dim(slots, (y + k) % 4, 1, keepdims=False) for k in range(4)
    ]
    along_y = [along_y[0]] + [shift(along_y[k], "y", k) for k in range(1, 4)]
    kept = jnp.where(core == x // 2, kept, given)
    along_z = [pick(kept, (z + k) % 4) for k in range(4)]
    for k in range(1, 4):
        along_z[k] = lax.ppermute(
            along_z[k],
            ALL,
            [(place(b, c, b, a), place((b + k) % 4, c, b, a)) for b, a in chips for c in range(2)],
        )

    lead_row = jnp.sum(
        jnp.where(slot[:, None, :] == jnp.arange(2)[None, :, None], groups[:, None, :] + 1, 0), axis=2
    ) - 1
    lead_row = jnp.where(lead_row < 8, lead_row, -1)
    lead_col = jnp.sum(jnp.where(columns < 8, columns + 1, 0), axis=2) - 1
    lead_col = jnp.repeat(lead_col, 4, axis=0)
    tile = jnp.where(
        (lead_row[:, None, :] >= 0) & (lead_col[:, :, None] >= 0),
        lead_row[:, None, :] * 8 + lead_col[:, :, None],
        -1,
    ).reshape(256)
    wanted = jnp.array([i * 8 + j for i, j in LOWER])
    spread = (tile[None, :] == wanted[:, None]).astype(BF16)
    lead = nn(spread, first[:, :2].reshape(256, T))
    lead_own = first[:16, 2:6].reshape(16, 8, 64).transpose(1, 0, 2).reshape(64, T)
    lead_own = jnp.concatenate([lead_own[8 * i : 8 * i + i + 1] for i in range(8)], axis=0)
    lead = jnp.broadcast_to((lead + lead_own.astype(F32))[None], (16, 36, T))

    lead = lax.all_to_all(lead, COL, 0, 0, tiled=True)
    by_shift = [lead] + [shift(lead, "z", k) for k in range(1, 4)]
    by_shift, along_y, along_z, packed = lax.optimization_barrier(
        (by_shift, along_y, along_z, packed)
    )
    here = lax.all_to_all(packed, ROW + ("x",), 0, 0, tiled=True).reshape(128, 64, T)
    own_q = jnp.where(z == y, along_z[0], 0) + along_z[1] + along_z[2] + along_z[3]
    own_q = own_q.reshape(2, 64, 8, T).transpose(2, 0, 1, 3).reshape(16, 64, T)
    parts = jnp.concatenate([jnp.stack(along_y).reshape(32, 64, T), own_q], axis=0)
    buf_q = lax.all_gather(parts, ROW, axis=0, tiled=False)
    lead = jnp.stack([select((z - n) % 4, *by_shift) for n in range(4)])
    other = swap(lead)
    lead = jnp.where(
        core == 0, jnp.stack([lead, other], axis=1), jnp.stack([other, lead], axis=1)
    ).reshape(128, 36, T).transpose(1, 0, 2)

    i1, i1h, i1l = panel_call(
        panel1_kernel, "panel1", 10, (F32, BF16, BF16), [(PW, PW), (T, T)], lead
    )
    i1, here = lax.optimization_barrier((i1, here))
    packed = pack_columns(here, column_orders.astype(I32).reshape(-1))
    tiles = lax.all_to_all(packed, COL, 0, 0, tiled=True).reshape(4, 2, 2, 8, 2, 64, T)
    i1, packed = lax.optimization_barrier((i1, packed))
    lh, ll, i2h, i2l = panel_call(
        panel2_kernel,
        "panel2",
        36,
        (BF16,) * 4,
        [(PW, PW), (PW, PW), (T, T), (PW, PW)],
        lead,
        i1,
    )

    by_child = groups.reshape(2, 64)
    ranks = rank.reshape(2, 4, 16)
    group = jnp.arange(4)[None, :, None]

    def find(first, count, values):
        hit = by_child[:, None, :] == (first + jnp.arange(count))[None, :, None]
        return jnp.sum(jnp.where(hit, values.reshape(2, 1, 64) + 1, 0), axis=2) - 1

    row_source = find(row * 16, 16, group * 2 + ranks).reshape(-1)
    col_source = find(col * 8, 8, group * 2 + ranks).reshape(-1)
    row_group = jnp.arange(8).reshape(2, 4, 1)
    q_rows = find(col * 8, 8, row_group * 32 + ranks * 2)
    r_rows = find(row * 16, 16, ranks * 32 + row_group * 2)
    q_cols = find(0, 8, (y - group) % 4 * 8 + ranks * 4)
    r_cols = find(0, 8, group * 64 + ranks)
    pat_rows = lax.dynamic_slice(pattern, (row * 16, 0), (16, 128))
    factor_tab = jnp.concatenate(
        [
            q_rows.T.reshape(-1),
            r_rows.T.reshape(-1),
            q_cols.reshape(-1),
            r_cols.reshape(-1),
            lax.dynamic_slice(pattern, (col * 8, 0), (8, 8)).reshape(-1),
            pat_rows[:, :8].reshape(-1),
            col * 8 + jnp.arange(8),
            row * 16 + jnp.arange(16),
            jnp.stack([8 + col]),
        ]
    ).astype(I32)
    update_tab = jnp.concatenate(
        [
            row_source,
            col_source,
            lax.dynamic_slice(pat_rows, (0, col * 8), (16, 8)).reshape(-1),
            jnp.stack([col]),
        ]
    ).astype(I32)
    high, low, fac = factor_rows(
        factor_tab, own_cols, buf_q, buf_r, (i1h, i1l, lh, ll, i2h, i2l)
    )
    return update(update_tab, high, low, own_cols, tiles), fac


def solution(mesh):
    grid = Mesh(mesh.devices.reshape(4, 2, 4, 4), ALL)
    return jax.shard_map(
        body,
        mesh=grid,
        in_specs=(P(ROW, COL), P(), P(), P(ROW, None)),
        out_specs=(P(ROW, COL), P(ALL, None)),
        check_vma=False,
    )
```

```python
import jax
import jax.numpy as jnp
from jax import lax
from jax.experimental import pallas as pl
from jax.experimental.pallas import tpu as pltpu
from jax.sharding import Mesh, PartitionSpec as P

F32 = jnp.float32
BF16 = jnp.bfloat16
I32 = jnp.int32
T = 128
PW = 512
ROW = ("z", "core")
COL = ("y", "x")
ALL = ROW + COL
FIRST = [(i, j) for i in range(4) for j in range(i + 1)]
LOWER = FIRST + [(i, j) for i in range(4, 8) for j in range(i + 1)]
HI = lax.Precision.HIGHEST
MIB = 2**20
VMEM = 56 * MIB


def nt(a, b, precision=None):
    return lax.dot_general(
        a, b, (((1,), (1,)), ((), ())), precision=precision, preferred_element_type=F32
    )


def nn(a, b, precision=None):
    return lax.dot_general(
        a, b, (((1,), (0,)), ((), ())), precision=precision, preferred_element_type=F32
    )


def halves(x):
    high = x.astype(BF16)
    return high, (x - high.astype(F32)).astype(BF16)


def nt3(a_high, a_low, b_high, b_low):
    return nt(a_high, b_high) + (nt(a_high, b_low) + nt(a_low, b_high))


def lanes(x, j):
    return jnp.broadcast_to(x[:, j : j + 1], x.shape)


def subs(x, i):
    return jnp.broadcast_to(x[i : i + 1, :], x.shape)


def rsqrt(d):
    return lax.rsqrt(d)


def invert_block(load, store):
    rest = [load(s) for s in range(16)]
    sub = lax.broadcasted_iota(I32, (8, T), 0)
    lane = lax.broadcasted_iota(I32, (8, T), 1)
    right = [(lane == sub + 8 * s).astype(F32) for s in range(16)]
    for s in range(16):
        col = [lanes(rest[s], 8 * s + t) for t in range(8)]
        a = {(i, t): subs(col[t], i) for t in range(8) for i in range(t, 8)}
        rs = []
        for t in range(8):
            rs.append(rsqrt(a[t, t]))
            for i in range(t + 1, 8):
                a[i, t] = a[i, t] * rs[t]
            for m in range(t + 1, 8):
                for i in range(m, 8):
                    a[i, m] = a[i, m] - a[i, t] * a[m, t]
        u, w = [], []
        for t in range(8):
            x, y = subs(rest[s], t), subs(right[s], t)
            for m in range(t):
                x = x - a[t, m] * u[m]
                y = y - a[t, m] * w[m]
            u.append(x * rs[t])
            w.append(y * rs[t])
        out = w[0]
        for t in range(1, 8):
            out = jnp.where(sub == t, w[t], out)
        store(s, out)
        for n in range(s + 1, 16):
            c = []
            for t in range(8):
                x = lanes(rest[n], 8 * s + t)
                for m in range(t):
                    x = x - a[t, m] * c[m]
                c.append(x * rs[t])
            x, y = rest[n], right[n]
            for t in range(8):
                x = x - c[t] * u[t]
                y = y - c[t] * w[t]
            rest[n], right[n] = x, y


def factor_panel(a, inv, out):
    out[...] = jnp.zeros((PW, PW), F32)

    def step(k, _):
        kk = pl.multiple_of(k * T, T)

        def load(s):
            return a[pl.ds(kk + 8 * s, 8), pl.ds(kk, T)]

        def store(s, v):
            inv[8 * s : 8 * s + 8, :] = v

        invert_block(load, store)
        for b in range(4):

            @pl.when(k == b)
            def _():
                lo, top = T * b, T * (b + 1)
                v = inv[...]
                if b:
                    out[lo:top, :lo] = nn(v, out[lo:top, :lo], HI)
                out[lo:top, lo:top] = v
                if b < 3:
                    col = nt(a[top:, lo:top], v, HI)
                    for j in range(b + 1, 4):
                        r = T * j
                        a[r:, r : r + T] -= nt(col[r - top :], col[r - top : r - top + T], HI)
                    out[top:, :top] -= nn(col, out[lo:top, :top], HI)

        return 0

    lax.fori_loop(0, 4, step, 0)


def panel1_kernel(lead_ref, i1_ref, i1h, i1l, a, inv):
    for n, (i, j) in enumerate(FIRST):
        a[i * T : i * T + T, j * T : j * T + T] = lead_ref[n]
    factor_panel(a, inv, i1_ref)
    i1h[...], i1l[...] = halves(i1_ref[...].T)


def panel2_kernel(lead_ref, i1_ref, lh, ll, i2h, i2l, a, low, inv, i2):
    for n, (i, j) in enumerate(LOWER):
        if i < 4:
            continue
        if j < 4:
            low[i * T - PW : i * T - PW + T, j * T : j * T + T] = lead_ref[n]
        else:
            a[i * T - PW : i * T - PW + T, j * T - PW : j * T - PW + T] = lead_ref[n]
    col = nt(low[...], i1_ref[...], HI)
    lh[...], ll[...] = halves(col.T)
    for j in range(4):
        r = T * j
        a[r:, r : r + T] -= nt(col[r:], col[r : r + T], HI)
    factor_panel(a, inv, i2)
    i2h[...], i2l[...] = halves(i2[...].T)


def panel_call(kernel, name, tiles, outs, scratch, lead, *args):
    whole = pl.BlockSpec((PW, PW), lambda i: (0, 0), pipeline_mode=pl.Buffered(1))
    return pl.pallas_call(
        kernel,
        out_shape=tuple(jax.ShapeDtypeStruct((PW, PW), t) for t in outs),
        grid=(1,),
        in_specs=[pl.BlockSpec((tiles, T, T), lambda i: (0, 0, 0), pipeline_mode=pl.Buffered(1))]
        + [whole] * len(args),
        out_specs=[whole] * len(outs),
        scratch_shapes=[pltpu.VMEM(x, F32) for x in scratch],
        compiler_params=pltpu.CompilerParams(vmem_limit_bytes=VMEM),
        cost_estimate=pl.CostEstimate(flops=25 * 10**9, bytes_accessed=4 * MIB, transcendentals=0),
        name=name,
    )(lead, *args)


def pack_rows_kernel(tab, top, low, out):
    for t, ref in enumerate((top, low)):
        for h in range(2):
            for k in range(4):
                out[t * 2 + h, k] = ref[64 * h : 64 * h + 64, k * T : k * T + T]


def pack_rows(children, order):
    return pl.pallas_call(
        pack_rows_kernel,
        out_shape=jax.ShapeDtypeStruct((32, 4, 64, T), BF16),
        grid_spec=pltpu.PrefetchScalarGridSpec(
            num_scalar_prefetch=1,
            grid=(8,),
            in_specs=[
                pl.BlockSpec((T, PW), lambda p, tab: (tab[2 * p], 0)),
                pl.BlockSpec((T, PW), lambda p, tab: (tab[2 * p + 1], 0)),
            ],
            out_specs=pl.BlockSpec((4, 4, 64, T), lambda p, tab: (p, 0, 0, 0)),
        ),
        compiler_params=pltpu.CompilerParams(vmem_limit_bytes=16 * MIB),
        cost_estimate=pl.CostEstimate(flops=0, bytes_accessed=4 * MIB, transcendentals=0),
        name="pack_rows",
    )(order, children, children)


def pack_columns_kernel(tab, ref, out):
    p = pl.program_id(0)
    for g in range(8):
        for s in range(2):
            part = ref[g * 16 + tab[g // 4 * 16 + p * 2 + s]]
            for q in range(2):
                out[q, g, s] = part


def pack_columns(halves_here, orders):
    return pl.pallas_call(
        pack_columns_kernel,
        out_shape=jax.ShapeDtypeStruct((16, 8, 2, 64, T), BF16),
        grid_spec=pltpu.PrefetchScalarGridSpec(
            num_scalar_prefetch=1,
            grid=(8,),
            in_specs=[
                pl.BlockSpec((128, 64, T), lambda p, tab: (0, 0, 0), pipeline_mode=pl.Buffered(1))
            ],
            out_specs=pl.BlockSpec((2, 8, 2, 64, T), lambda p, tab: (p, 0, 0, 0, 0)),
        ),
        compiler_params=pltpu.CompilerParams(vmem_limit_bytes=16 * MIB),
        cost_estimate=pl.CostEstimate(flops=0, bytes_accessed=6 * MIB, transcendentals=0),
        name="pack_columns",
    )(orders, halves_here)


TM = 512
SUB = 128
QS = 1024 // TM
RS = 2048 // TM
G = TM // T
STEPS = QS + RS
F_ROW, F_COL, F_PAT, F_AT, F_SHARE = 0, 48, 80, 272, 296


def nn3(a_high, a_low, b_high, b_low):
    return nn(jnp.concatenate([a_high, a_high, a_low], axis=1), jnp.concatenate([b_high, b_low, b_high], axis=0))


def factor_kernel(
    tab, own_q, own_r, buf_q, buf_r, i1h, i1l, lh, ll, i2h, i2l, high, low, fac, sh, sl, rest, tiles, sem
):
    step = pl.program_id(0)

    def load(n):
        ref = (buf_q.at[:, pl.ds(0, 32)], buf_r)[n]
        return pltpu.make_async_copy(ref, tiles.at[pl.ds(8 * n, 8)], sem.at[n])

    def assemble(i, slot, g):
        side = (i >= QS).astype(I32)
        stride = jnp.where(side == 1, 16, 1)
        n = i * G + g
        for j in range(8):
            kept = tab[F_PAT + n * 8 + j] != 0
            at = [(tab[F_ROW + n * 2 + c], tab[F_COL + side * 16 + c * 8 + j]) for c in range(2)]
            valid = [jnp.logical_and(a >= 0, b >= 0) for a, b in at]
            at = [side * 256 + a + b for a, b in at]
            for h in range(2):
                line = slice(g * T + 64 * h, g * T + 64 * h + 64)
                x = jnp.where(side == 1, own_r[line, j * T : j * T + T], own_q[g, j * 2 + h])
                x = jnp.where(kept, x, jnp.zeros_like(x)).astype(F32)
                for c in range(2):
                    half = jnp.where(valid[c], at[c] + h * stride, 512)
                    x = x + tiles[half // 32, half % 32].astype(F32)
                if j < 4:
                    place = slice(j * T, j * T + T)
                    sh[slot, line, place], sl[slot, line, place] = halves(x)
                else:
                    rest[slot, line, j * T - PW : j * T - PW + T] = x

    def by_inverse(xh, xl, ih, il):
        left = nn3(xh[:, :256], xl[:, :256], ih[:256, :256], il[:256, :256])
        right = nn3(xh, xl, ih[:, 256:], il[:, 256:])
        return jnp.concatenate([left, right], axis=1)

    def multiply(i, slot, between):
        count, lines = TM // SUB, SUB // T
        zero = jnp.zeros((T, PW), BF16)
        at = [slice(c * SUB, c * SUB + SUB) for c in range(count)]
        f0 = [by_inverse(sh[slot, x], sl[slot, x], i1h, i1l) for x in at]
        between(0)
        ups, f1 = [], []
        for c in range(count):
            f0h, f0l = halves(f0[c])
            ups.append(nn3(f0h, f0l, lh[...], ll[...]))
            for g in range(lines):
                first = tab[F_AT + i * G + c * lines + g]
                line, to = slice(g * T, g * T + T), slice(c * SUB + g * T, c * SUB + g * T + T)
                high[to, :PW] = jnp.where(first >= 4, f0h[line], zero)
                low[to, :PW] = jnp.where(first >= 4, f0l[line], zero)
        between(1)
        for c in range(count):
            rows = []
            for g in range(lines):
                n = i * G + c * lines + g
                line = slice(g * T, g * T + T)
                row = []
                for j in range(4):
                    keep = jnp.logical_and(tab[F_PAT + n * 8 + 4 + j] != 0, tab[F_AT + n] >= 4)
                    part = ups[c][line, j * T : j * T + T]
                    old = rest[slot, c * SUB + g * T : c * SUB + g * T + T, j * T : j * T + T]
                    row.append(old - jnp.where(keep, part, 0.0))
                rows.append(jnp.concatenate(row, axis=1))
            f1.append(by_inverse(*halves(jnp.concatenate(rows, axis=0)), i2h, i2l))
        between(2)
        for c in range(count):
            f1h, f1l = halves(f1[c])
            for g in range(lines):
                first = tab[F_AT + i * G + c * lines + g]
                line, to = slice(g * T, g * T + T), slice(c * SUB + g * T, c * SUB + g * T + T)
                high[to, PW:] = jnp.where(first >= 8, f1h[line], zero)
                low[to, PW:] = jnp.where(first >= 8, f1l[line], zero)
        return list(zip(f0, f1))

    @pl.when(step == 0)
    def _():
        load(0).start()
        load(1).start()
        tiles[16, 0] = jnp.zeros((64, T), BF16)
        load(0).wait()
        load(1).wait()
        for g in range(G):
            assemble(step, 0, g)

    @pl.when(step > 0)
    def _():
        slot = step % 2
        nxt = jnp.minimum(step, STEPS - 1)

        def between(k):
            for g in range(G):
                if g * 3 // G == k:
                    assemble(nxt, slot, g)

        keep = multiply(step - 1, 1 - slot, between)
        for g in range(G):
            c, e = divmod(g, SUB // T)

            @pl.when(tab[F_SHARE] == (step - 1) * G + g)
            def _():
                f0, f1 = keep[c]
                fac[:, :PW] = f0[e * T : e * T + T]
                fac[:, PW:] = jnp.where(tab[F_AT + (step - 1) * G + g] >= 4, f1[e * T : e * T + T], 0.0)


def factor_rows(tab, own_r, buf_q, buf_r, inverses):
    small = pl.BlockSpec((PW, PW), lambda i, tab: (0, 0), pipeline_mode=pl.Buffered(1))
    out = pl.BlockSpec((TM, 1024), lambda i, tab: (jnp.maximum(i - 1, 0), 0))
    shape = jax.ShapeDtypeStruct((3072, 1024), BF16)
    return pl.pallas_call(
        factor_kernel,
        out_shape=(shape, shape, jax.ShapeDtypeStruct((T, 1024), F32)),
        grid_spec=pltpu.PrefetchScalarGridSpec(
            num_scalar_prefetch=1,
            grid=(STEPS + 1,),
            in_specs=[
                pl.BlockSpec((G, 16, 64, T), lambda i, tab: (jnp.minimum(i, QS - 1), 2, 0, 0)),
                pl.BlockSpec((TM, 1024), lambda i, tab: (jnp.clip(i - QS, 0, RS - 1), 0)),
                pl.BlockSpec(memory_space=pl.ANY),
                pl.BlockSpec(memory_space=pl.ANY),
            ]
            + [small] * 6,
            out_specs=[out, out, pl.BlockSpec((T, 1024), lambda i, tab: (0, 0))],
            scratch_shapes=[
                pltpu.VMEM((2, TM, PW), BF16),
                pltpu.VMEM((2, TM, PW), BF16),
                pltpu.VMEM((2, TM, PW), F32),
                pltpu.VMEM((17, 32, 64, T), BF16),
                pltpu.SemaphoreType.DMA((2,)),
            ],
        ),
        compiler_params=pltpu.CompilerParams(vmem_limit_bytes=VMEM),
        cost_estimate=pl.CostEstimate(
            flops=16 * 10**9, bytes_accessed=30 * MIB, transcendentals=0
        ),
        name="factor_rows",
    )(tab, buf_q, own_r, buf_q, buf_r.reshape(8, 32, 64, T), *inverses)


UM = 256
UG = UM // T
U_ROW, U_COL, U_PAT, U_LEFT = 0, 32, 48, 176


def update_kernel(tab, qh, ql, rh, rl, own, *rest):
    bufs, out = rest[: 2 * UG], rest[2 * UG]
    n = pl.program_id(0) * UG
    at_left = tab[U_LEFT] == 0
    fh, fl = rh[...], rl[...]
    f3 = jnp.concatenate([fh, fh, fl], axis=1)
    for h in range(4):
        qr = slice(h * 256, h * 256 + 256)
        up = nt(f3, jnp.concatenate([qh[qr, :], ql[qr, :], qh[qr, :]], axis=1))
        for g in range(UG):
            for e in range(2):
                j = h * 2 + e
                at = slice(g * T, g * T + T), slice(j * T, j * T + T)
                x = jnp.where(at_left, own[at].astype(F32), 0.0)
                for c in range(2):
                    cs = tab[U_COL + c * 8 + j]
                    valid = jnp.logical_and(tab[U_ROW + c * 16 + n + g] >= 0, cs >= 0)
                    cs = jnp.maximum(cs, 0)
                    tile = jnp.concatenate(
                        [bufs[g * 2 + c][cs // 2, 0, i, 0, cs % 2] for i in range(2)], axis=0
                    )
                    x = x + jnp.where(valid, tile.astype(F32), 0.0)
                x = x - up[g * T : g * T + T, e * T : e * T + T]
                kept = tab[U_PAT + (n + g) * 8 + j] != 0
                out[at] = jnp.where(kept, x, 0.0).astype(BF16)


def update(tab, high, low, own, buf):
    once = pl.Buffered(1)
    block = pl.BlockSpec((UM, 1024), lambda i, tab: (i, 0))
    after = pl.BlockSpec((UM, 1024), lambda i, tab: (i + 1024 // UM, 0))

    def tiles(g, c):
        def at(i, tab):
            rs = jnp.maximum(tab[U_ROW + c * 16 + i * UG + g], 0)
            return 0, rs % 2, 0, c * 4 + rs // 2, 0, 0, 0

        return pl.BlockSpec((4, 1, 2, 1, 2, 64, T), at)

    whole = pl.BlockSpec((1024, 1024), lambda i, tab: (0, 0), pipeline_mode=once)
    return pl.pallas_call(
        update_kernel,
        out_shape=jax.ShapeDtypeStruct((2048, 1024), BF16),
        grid_spec=pltpu.PrefetchScalarGridSpec(
            num_scalar_prefetch=1,
            grid=(2048 // UM,),
            in_specs=[whole, whole, after, after, block]
            + [tiles(g, c) for g in range(UG) for c in range(2)],
            out_specs=block,
        ),
        compiler_params=pltpu.CompilerParams(vmem_limit_bytes=VMEM),
        cost_estimate=pl.CostEstimate(
            flops=13 * 10**9, bytes_accessed=36 * MIB, transcendentals=0
        ),
        name="update",
    )(tab, high, low, high, low, own, *([buf] * (2 * UG)))


def shift(x, axis, k):
    return lax.ppermute(x, axis, [(i, (i + k) % 4) for i in range(4)])


def swap(x):
    return lax.ppermute(x, "core", [(0, 1), (1, 0)])


def pick(x, n):
    return lax.dynamic_index_in_dim(x, n, 0, keepdims=False)


def select(n, *cases):
    return lax.select_n(n, *cases)


def body(children, child_maps, pattern, own_cols):
    z, core, y, x = (lax.axis_index(a) for a in ALL)
    row, col = z * 2 + core, y * 4 + x
    child = row // 4

    groups = child_maps.reshape(8, 16)
    home = groups // 16
    earlier = jnp.arange(16)[None, :] < jnp.arange(16)[:, None]
    rank = jnp.sum(((home[:, :, None] == home[:, None, :]) & earlier[None]).astype(I32), axis=2)
    slot = home * 2 + rank
    orders = jnp.sum(
        jnp.where(
            slot[:, None, :] == jnp.arange(16)[None, :, None], jnp.arange(16)[None, None, :], 0
        ),
        axis=2,
    )
    order = pick(orders, row)
    column_orders = pick(orders.reshape(2, 4, 16).transpose(1, 0, 2), y)
    columns = child_maps.reshape(2, 16, 4)
    mine_columns = pick(pick(columns, child), col)
    strip_at = jnp.sum(jnp.where(mine_columns < 8, jnp.arange(4), 0))

    mine = lax.dynamic_slice(children, (0, strip_at * T), (2048, T)).reshape(16, T, T)[order]
    from_x = column_orders[:, :2] // 4

    strip = lax.all_to_all(mine.reshape(32, 64, T), ROW + ("x",), 0, 0, tiled=True)
    packed = pack_rows(children, order.astype(I32))
    own_piece = lax.dynamic_slice(own_cols, (0, col * 64), (1024, 64))
    own_piece = own_piece.reshape(8, T, 64).transpose(1, 0, 2).reshape(T, 4, T)
    first = jnp.concatenate(
        [mine[:2].transpose(1, 0, 2), own_piece, jnp.zeros((T, 2, T), BF16)], axis=1
    )
    by_half = mine.reshape(4, 2, 2, T, T)
    along_x = [
        lax.dynamic_index_in_dim(by_half, (x + k) % 4 // 2, 1, keepdims=False) for k in range(4)
    ]
    halved = pick(own_cols.reshape(2, 4, 2, T, 1024), x % 2)
    kept = lax.dynamic_index_in_dim(halved, core, 1, keepdims=False)
    given = lax.dynamic_index_in_dim(halved, 1 - core, 1, keepdims=False)
    place = lambda z, c, y, x: ((z * 2 + c) * 4 + y) * 4 + x
    chips = [(y, x) for y in range(4) for x in range(4)]
    along_x, given, first, strip = lax.optimization_barrier((along_x, given, first, strip))
    strip = jnp.take_along_axis(
        strip.reshape(2, 4, 4, 64, T), from_x[:, None, :, None, None], axis=2
    )
    buf_r = lax.all_gather(strip, COL, axis=0, tiled=False).reshape(256, 64, T)
    first = lax.all_to_all(first, ALL, 0, 0, tiled=True)
    along_x = [along_x[0]] + [shift(along_x[k], "x", k) for k in range(1, 4)]
    given = lax.ppermute(
        given, ALL, [(place(b, a // 2, b, a), place(b, 1 - a // 2, b, a)) for b, a in chips]
    )
    steps = (x - pick(from_x, child)) % 4
    slots = jnp.stack([select(steps[s], *along_x) for s in range(2)])
    along_y = [
        lax.dynamic_index_in_dim(slots, (y + k) % 4, 1, keepdims=False) for k in range(4)
    ]
    along_y = [along_y[0]] + [shift(along_y[k], "y", k) for k in range(1, 4)]
    kept = jnp.where(core == x // 2, kept, given)
    along_z = [pick(kept, (z + k) % 4) for k in range(4)]
    for k in range(1, 4):
        along_z[k] = lax.ppermute(
            along_z[k],
            ALL,
            [(place(b, c, b, a), place((b + k) % 4, c, b, a)) for b, a in chips for c in range(2)],
        )

    lead_row = jnp.sum(
        jnp.where(slot[:, None, :] == jnp.arange(2)[None, :, None], groups[:, None, :] + 1, 0), axis=2
    ) - 1
    lead_row = jnp.where(lead_row < 8, lead_row, -1)
    lead_col = jnp.sum(jnp.where(columns < 8, columns + 1, 0), axis=2) - 1
    lead_col = jnp.repeat(lead_col, 4, axis=0)
    tile = jnp.where(
        (lead_row[:, None, :] >= 0) & (lead_col[:, :, None] >= 0),
        lead_row[:, None, :] * 8 + lead_col[:, :, None],
        -1,
    ).reshape(256)
    wanted = jnp.array([i * 8 + j for i, j in LOWER])
    spread = (tile[None, :] == wanted[:, None]).astype(BF16)
    lead = nn(spread, first[:, :2].reshape(256, T))
    lead_own = first[:16, 2:6].reshape(16, 8, 64).transpose(1, 0, 2).reshape(64, T)
    lead_own = jnp.concatenate([lead_own[8 * i : 8 * i + i + 1] for i in range(8)], axis=0)
    lead = jnp.broadcast_to((lead + lead_own.astype(F32))[None], (16, 36, T))

    lead = lax.all_to_all(lead, COL, 0, 0, tiled=True)
    by_shift = [lead] + [shift(lead, "z", k) for k in range(1, 4)]
    by_shift, along_y, along_z, packed = lax.optimization_barrier(
        (by_shift, along_y, along_z, packed)
    )
    here = lax.all_to_all(packed, ROW + ("x",), 0, 0, tiled=True).reshape(128, 64, T)
    own_q = jnp.where(z == y, along_z[0], 0) + along_z[1] + along_z[2] + along_z[3]
    own_q = own_q.reshape(2, 64, 8, T).transpose(2, 0, 1, 3).reshape(16, 64, T)
    parts = jnp.concatenate([jnp.stack(along_y).reshape(32, 64, T), own_q], axis=0)
    buf_q = lax.all_gather(parts, ROW, axis=0, tiled=False)
    lead = jnp.stack([select((z - n) % 4, *by_shift) for n in range(4)])
    other = swap(lead)
    lead = jnp.where(
        core == 0, jnp.stack([lead, other], axis=1), jnp.stack([other, lead], axis=1)
    ).reshape(128, 36, T).transpose(1, 0, 2)

    i1, i1h, i1l = panel_call(
        panel1_kernel, "panel1", 10, (F32, BF16, BF16), [(PW, PW), (T, T)], lead
    )
    i1, here = lax.optimization_barrier((i1, here))
    packed = pack_columns(here, column_orders.astype(I32).reshape(-1))
    tiles = lax.all_to_all(packed, COL, 0, 0, tiled=True).reshape(4, 2, 2, 8, 2, 64, T)
    i1, packed = lax.optimization_barrier((i1, packed))
    lh, ll, i2h, i2l = panel_call(
        panel2_kernel,
        "panel2",
        36,
        (BF16,) * 4,
        [(PW, PW), (PW, PW), (T, T), (PW, PW)],
        lead,
        i1,
    )

    by_child = groups.reshape(2, 64)
    ranks = rank.reshape(2, 4, 16)
    group = jnp.arange(4)[None, :, None]

    def find(first, count, values):
        hit = by_child[:, None, :] == (first + jnp.arange(count))[None, :, None]
        return jnp.sum(jnp.where(hit, values.reshape(2, 1, 64) + 1, 0), axis=2) - 1

    row_source = find(row * 16, 16, group * 2 + ranks).reshape(-1)
    col_source = find(col * 8, 8, group * 2 + ranks).reshape(-1)
    row_group = jnp.arange(8).reshape(2, 4, 1)
    q_rows = find(col * 8, 8, row_group * 32 + ranks * 2)
    r_rows = find(row * 16, 16, ranks * 32 + row_group * 2)
    q_cols = find(0, 8, (y - group) % 4 * 8 + ranks * 4)
    r_cols = find(0, 8, group * 64 + ranks)
    pat_rows = lax.dynamic_slice(pattern, (row * 16, 0), (16, 128))
    factor_tab = jnp.concatenate(
        [
            q_rows.T.reshape(-1),
            r_rows.T.reshape(-1),
            q_cols.reshape(-1),
            r_cols.reshape(-1),
            lax.dynamic_slice(pattern, (col * 8, 0), (8, 8)).reshape(-1),
            pat_rows[:, :8].reshape(-1),
            col * 8 + jnp.arange(8),
            row * 16 + jnp.arange(16),
            jnp.stack([8 + col]),
        ]
    ).astype(I32)
    update_tab = jnp.concatenate(
        [
            row_source,
            col_source,
            lax.dynamic_slice(pat_rows, (0, col * 8), (16, 8)).reshape(-1),
            jnp.stack([col]),
        ]
    ).astype(I32)
    high, low, fac = factor_rows(
        factor_tab, own_cols, buf_q, buf_r, (i1h, i1l, lh, ll, i2h, i2l)
    )
    return update(update_tab, high, low, own_cols, tiles), fac


def solution(mesh):
    grid = Mesh(mesh.devices.reshape(4, 2, 4, 4), ALL)
    return jax.shard_map(
        body,
        mesh=grid,
        in_specs=(P(ROW, COL), P(), P(), P(ROW, None)),
        out_specs=(P(ROW, COL), P(ALL, None)),
        check_vma=False,
    )
```

```python
import jax
import jax.numpy as jnp
from jax import lax
from jax.experimental import pallas as pl
from jax.experimental.pallas import tpu as pltpu
from jax.sharding import Mesh, PartitionSpec as P

F32 = jnp.float32
BF16 = jnp.bfloat16
I32 = jnp.int32
T = 128
PW = 512
ROW = ("z", "core")
COL = ("y", "x")
ALL = ROW + COL
FIRST = [(i, j) for i in range(4) for j in range(i + 1)]
LOWER = FIRST + [(i, j) for i in range(4, 8) for j in range(i + 1)]
HI = lax.Precision.HIGHEST
MIB = 2**20
VMEM = 56 * MIB


def nt(a, b, precision=None):
    return lax.dot_general(
        a, b, (((1,), (1,)), ((), ())), precision=precision, preferred_element_type=F32
    )


def nn(a, b, precision=None):
    return lax.dot_general(
        a, b, (((1,), (0,)), ((), ())), precision=precision, preferred_element_type=F32
    )


def halves(x):
    high = x.astype(BF16)
    return high, (x - high.astype(F32)).astype(BF16)


def nt3(a_high, a_low, b_high, b_low):
    return nt(a_high, b_high) + (nt(a_high, b_low) + nt(a_low, b_high))


def lanes(x, j):
    return jnp.broadcast_to(x[:, j : j + 1], x.shape)


def subs(x, i):
    return jnp.broadcast_to(x[i : i + 1, :], x.shape)


def rsqrt(d):
    return lax.rsqrt(d)


def invert_block(load, store):
    rest = [load(s) for s in range(16)]
    sub = lax.broadcasted_iota(I32, (8, T), 0)
    lane = lax.broadcasted_iota(I32, (8, T), 1)
    right = [(lane == sub + 8 * s).astype(F32) for s in range(16)]
    for s in range(16):
        col = [lanes(rest[s], 8 * s + t) for t in range(8)]
        a = {(i, t): subs(col[t], i) for t in range(8) for i in range(t, 8)}
        rs = []
        for t in range(8):
            rs.append(rsqrt(a[t, t]))
            for i in range(t + 1, 8):
                a[i, t] = a[i, t] * rs[t]
            for m in range(t + 1, 8):
                for i in range(m, 8):
                    a[i, m] = a[i, m] - a[i, t] * a[m, t]
        u, w = [], []
        for t in range(8):
            x, y = subs(rest[s], t), subs(right[s], t)
            for m in range(t):
                x = x - a[t, m] * u[m]
                y = y - a[t, m] * w[m]
            u.append(x * rs[t])
            w.append(y * rs[t])
        out = w[0]
        for t in range(1, 8):
            out = jnp.where(sub == t, w[t], out)
        store(s, out)
        for n in range(s + 1, 16):
            c = []
            for t in range(8):
                x = lanes(rest[n], 8 * s + t)
                for m in range(t):
                    x = x - a[t, m] * c[m]
                c.append(x * rs[t])
            x, y = rest[n], right[n]
            for t in range(8):
                x = x - c[t] * u[t]
                y = y - c[t] * w[t]
            rest[n], right[n] = x, y


def factor_panel(a, inv, out):
    out[...] = jnp.zeros((PW, PW), F32)

    def step(k, _):
        kk = pl.multiple_of(k * T, T)

        def load(s):
            return a[pl.ds(kk + 8 * s, 8), pl.ds(kk, T)]

        def store(s, v):
            inv[8 * s : 8 * s + 8, :] = v

        invert_block(load, store)
        for b in range(4):

            @pl.when(k == b)
            def _():
                lo, top = T * b, T * (b + 1)
                v = inv[...]
                if b:
                    out[lo:top, :lo] = nn(v, out[lo:top, :lo], HI)
                out[lo:top, lo:top] = v
                if b < 3:
                    col = nt(a[top:, lo:top], v, HI)
                    for j in range(b + 1, 4):
                        r = T * j
                        a[r:, r : r + T] -= nt(col[r - top :], col[r - top : r - top + T], HI)
                    out[top:, :top] -= nn(col, out[lo:top, :top], HI)

        return 0

    lax.fori_loop(0, 4, step, 0)


def panel1_kernel(lead_ref, i1_ref, i1h, i1l, a, inv):
    for n, (i, j) in enumerate(FIRST):
        a[i * T : i * T + T, j * T : j * T + T] = lead_ref[n]
    factor_panel(a, inv, i1_ref)
    i1h[...], i1l[...] = halves(i1_ref[...].T)


def panel2_kernel(lead_ref, i1_ref, lh, ll, i2h, i2l, a, low, inv, i2):
    for n, (i, j) in enumerate(LOWER):
        if i < 4:
            continue
        if j < 4:
            low[i * T - PW : i * T - PW + T, j * T : j * T + T] = lead_ref[n]
        else:
            a[i * T - PW : i * T - PW + T, j * T - PW : j * T - PW + T] = lead_ref[n]
    col = nt(low[...], i1_ref[...], HI)
    lh[...], ll[...] = halves(col.T)
    for j in range(4):
        r = T * j
        a[r:, r : r + T] -= nt(col[r:], col[r : r + T], HI)
    factor_panel(a, inv, i2)
    i2h[...], i2l[...] = halves(i2[...].T)


def panel_call(kernel, name, tiles, outs, scratch, lead, *args):
    whole = pl.BlockSpec((PW, PW), lambda i: (0, 0), pipeline_mode=pl.Buffered(1))
    return pl.pallas_call(
        kernel,
        out_shape=tuple(jax.ShapeDtypeStruct((PW, PW), t) for t in outs),
        grid=(1,),
        in_specs=[pl.BlockSpec((tiles, T, T), lambda i: (0, 0, 0), pipeline_mode=pl.Buffered(1))]
        + [whole] * len(args),
        out_specs=[whole] * len(outs),
        scratch_shapes=[pltpu.VMEM(x, F32) for x in scratch],
        compiler_params=pltpu.CompilerParams(vmem_limit_bytes=VMEM),
        cost_estimate=pl.CostEstimate(flops=25 * 10**9, bytes_accessed=4 * MIB, transcendentals=0),
        name=name,
    )(lead, *args)


def pack_rows_kernel(tab, top, low, out):
    for t, ref in enumerate((top, low)):
        for h in range(2):
            for k in range(4):
                out[t * 2 + h, k] = ref[64 * h : 64 * h + 64, k * T : k * T + T]


def pack_rows(children, order):
    return pl.pallas_call(
        pack_rows_kernel,
        out_shape=jax.ShapeDtypeStruct((32, 4, 64, T), BF16),
        grid_spec=pltpu.PrefetchScalarGridSpec(
            num_scalar_prefetch=1,
            grid=(8,),
            in_specs=[
                pl.BlockSpec((T, PW), lambda p, tab: (tab[2 * p], 0)),
                pl.BlockSpec((T, PW), lambda p, tab: (tab[2 * p + 1], 0)),
            ],
            out_specs=pl.BlockSpec((4, 4, 64, T), lambda p, tab: (p, 0, 0, 0)),
        ),
        compiler_params=pltpu.CompilerParams(vmem_limit_bytes=16 * MIB),
        cost_estimate=pl.CostEstimate(flops=0, bytes_accessed=4 * MIB, transcendentals=0),
        name="pack_rows",
    )(order, children, children)


def pack_columns_kernel(tab, ref, out):
    p = pl.program_id(0)
    for g in range(8):
        for s in range(2):
            part = ref[g * 16 + tab[g // 4 * 16 + p * 2 + s]]
            for q in range(2):
                out[q, g, s] = part


def pack_columns(halves_here, orders):
    return pl.pallas_call(
        pack_columns_kernel,
        out_shape=jax.ShapeDtypeStruct((16, 8, 2, 64, T), BF16),
        grid_spec=pltpu.PrefetchScalarGridSpec(
            num_scalar_prefetch=1,
            grid=(8,),
            in_specs=[
                pl.BlockSpec((128, 64, T), lambda p, tab: (0, 0, 0), pipeline_mode=pl.Buffered(1))
            ],
            out_specs=pl.BlockSpec((2, 8, 2, 64, T), lambda p, tab: (p, 0, 0, 0, 0)),
        ),
        compiler_params=pltpu.CompilerParams(vmem_limit_bytes=16 * MIB),
        cost_estimate=pl.CostEstimate(flops=0, bytes_accessed=6 * MIB, transcendentals=0),
        name="pack_columns",
    )(orders, halves_here)


TM = 512
SUB = 128
QS = 1024 // TM
RS = 2048 // TM
G = TM // T
STEPS = QS + RS
F_ROW, F_COL, F_PAT, F_AT, F_SHARE = 0, 48, 80, 272, 296


def nn3(a_high, a_low, b_high, b_low):
    return nn(jnp.concatenate([a_high, a_high, a_low], axis=1), jnp.concatenate([b_high, b_low, b_high], axis=0))


def factor_kernel(
    tab, own_q, own_r, buf_q, buf_r, i1h, i1l, lh, ll, i2h, i2l, high, low, fac, sh, sl, rest, tiles, sem
):
    step = pl.program_id(0)

    def load(n):
        ref = (buf_q.at[:, pl.ds(0, 32)], buf_r)[n]
        return pltpu.make_async_copy(ref, tiles.at[pl.ds(8 * n, 8)], sem.at[n])

    def assemble(i, slot, g):
        side = (i >= QS).astype(I32)
        stride = jnp.where(side == 1, 16, 1)
        n = i * G + g
        for j in range(8):
            kept = tab[F_PAT + n * 8 + j] != 0
            at = [(tab[F_ROW + n * 2 + c], tab[F_COL + side * 16 + c * 8 + j]) for c in range(2)]
            valid = [jnp.logical_and(a >= 0, b >= 0) for a, b in at]
            at = [side * 256 + a + b for a, b in at]
            for h in range(2):
                line = slice(g * T + 64 * h, g * T + 64 * h + 64)
                x = jnp.where(side == 1, own_r[line, j * T : j * T + T], own_q[g, j * 2 + h])
                x = jnp.where(kept, x, jnp.zeros_like(x)).astype(F32)
                for c in range(2):
                    half = jnp.where(valid[c], at[c] + h * stride, 512)
                    x = x + tiles[half // 32, half % 32].astype(F32)
                if j < 4:
                    place = slice(j * T, j * T + T)
                    sh[slot, line, place], sl[slot, line, place] = halves(x)
                else:
                    rest[slot, line, j * T - PW : j * T - PW + T] = x

    def by_inverse(xh, xl, ih, il):
        left = nn3(xh[:, :256], xl[:, :256], ih[:256, :256], il[:256, :256])
        right = nn3(xh, xl, ih[:, 256:], il[:, 256:])
        return jnp.concatenate([left, right], axis=1)

    def multiply(i, slot, between):
        count, lines = TM // SUB, SUB // T
        zero = jnp.zeros((T, PW), BF16)
        at = [slice(c * SUB, c * SUB + SUB) for c in range(count)]
        f0 = [by_inverse(sh[slot, x], sl[slot, x], i1h, i1l) for x in at]
        between(0)
        ups, f1 = [], []
        for c in range(count):
            f0h, f0l = halves(f0[c])
            ups.append(nn3(f0h, f0l, lh[...], ll[...]))
            for g in range(lines):
                first = tab[F_AT + i * G + c * lines + g]
                line, to = slice(g * T, g * T + T), slice(c * SUB + g * T, c * SUB + g * T + T)
                high[to, :PW] = jnp.where(first >= 4, f0h[line], zero)
                low[to, :PW] = jnp.where(first >= 4, f0l[line], zero)
        between(1)
        for c in range(count):
            rows = []
            for g in range(lines):
                n = i * G + c * lines + g
                line = slice(g * T, g * T + T)
                row = []
                for j in range(4):
                    keep = jnp.logical_and(tab[F_PAT + n * 8 + 4 + j] != 0, tab[F_AT + n] >= 4)
                    part = ups[c][line, j * T : j * T + T]
                    old = rest[slot, c * SUB + g * T : c * SUB + g * T + T, j * T : j * T + T]
                    row.append(old - jnp.where(keep, part, 0.0))
                rows.append(jnp.concatenate(row, axis=1))
            f1.append(by_inverse(*halves(jnp.concatenate(rows, axis=0)), i2h, i2l))
        between(2)
        for c in range(count):
            f1h, f1l = halves(f1[c])
            for g in range(lines):
                first = tab[F_AT + i * G + c * lines + g]
                line, to = slice(g * T, g * T + T), slice(c * SUB + g * T, c * SUB + g * T + T)
                high[to, PW:] = jnp.where(first >= 8, f1h[line], zero)
                low[to, PW:] = jnp.where(first >= 8, f1l[line], zero)
        return list(zip(f0, f1))

    @pl.when(step == 0)
    def _():
        load(0).start()
        load(1).start()
        tiles[16, 0] = jnp.zeros((64, T), BF16)
        load(0).wait()
        load(1).wait()
        for g in range(G):
            assemble(step, 0, g)

    @pl.when(step > 0)
    def _():
        slot = step % 2
        nxt = jnp.minimum(step, STEPS - 1)

        def between(k):
            for g in range(G):
                if g * 3 // G == k:
                    assemble(nxt, slot, g)

        keep = multiply(step - 1, 1 - slot, between)
        for g in range(G):
            c, e = divmod(g, SUB // T)

            @pl.when(tab[F_SHARE] == (step - 1) * G + g)
            def _():
                f0, f1 = keep[c]
                fac[:, :PW] = f0[e * T : e * T + T]
                fac[:, PW:] = jnp.where(tab[F_AT + (step - 1) * G + g] >= 4, f1[e * T : e * T + T], 0.0)


def factor_rows(tab, own_r, buf_q, buf_r, inverses):
    small = pl.BlockSpec((PW, PW), lambda i, tab: (0, 0), pipeline_mode=pl.Buffered(1))
    out = pl.BlockSpec((TM, 1024), lambda i, tab: (jnp.maximum(i - 1, 0), 0))
    shape = jax.ShapeDtypeStruct((3072, 1024), BF16)
    return pl.pallas_call(
        factor_kernel,
        out_shape=(shape, shape, jax.ShapeDtypeStruct((T, 1024), F32)),
        grid_spec=pltpu.PrefetchScalarGridSpec(
            num_scalar_prefetch=1,
            grid=(STEPS + 1,),
            in_specs=[
                pl.BlockSpec((G, 16, 64, T), lambda i, tab: (jnp.minimum(i, QS - 1), 2, 0, 0)),
                pl.BlockSpec((TM, 1024), lambda i, tab: (jnp.clip(i - QS, 0, RS - 1), 0)),
                pl.BlockSpec(memory_space=pl.ANY),
                pl.BlockSpec(memory_space=pl.ANY),
            ]
            + [small] * 6,
            out_specs=[out, out, pl.BlockSpec((T, 1024), lambda i, tab: (0, 0))],
            scratch_shapes=[
                pltpu.VMEM((2, TM, PW), BF16),
                pltpu.VMEM((2, TM, PW), BF16),
                pltpu.VMEM((2, TM, PW), F32),
                pltpu.VMEM((17, 32, 64, T), BF16),
                pltpu.SemaphoreType.DMA((2,)),
            ],
        ),
        compiler_params=pltpu.CompilerParams(vmem_limit_bytes=VMEM),
        cost_estimate=pl.CostEstimate(
            flops=16 * 10**9, bytes_accessed=30 * MIB, transcendentals=0
        ),
        name="factor_rows",
    )(tab, buf_q, own_r, buf_q, buf_r.reshape(8, 32, 64, T), *inverses)


UM = 256
UG = UM // T
U_ROW, U_COL, U_PAT, U_LEFT = 0, 32, 48, 176


def update_kernel(tab, qh, ql, rh, rl, own, *rest):
    bufs, out = rest[: 2 * UG], rest[2 * UG]
    n = pl.program_id(0) * UG
    at_left = tab[U_LEFT] == 0
    fh, fl = rh[...], rl[...]
    f3 = jnp.concatenate([fh, fh, fl], axis=1)
    for h in range(4):
        qr = slice(h * 256, h * 256 + 256)
        up = nt(f3, jnp.concatenate([qh[qr, :], ql[qr, :], qh[qr, :]], axis=1))
        for g in range(UG):
            for e in range(2):
                j = h * 2 + e
                at = slice(g * T, g * T + T), slice(j * T, j * T + T)
                x = jnp.where(at_left, own[at].astype(F32), 0.0)
                for c in range(2):
                    cs = tab[U_COL + c * 8 + j]
                    valid = jnp.logical_and(tab[U_ROW + c * 16 + n + g] >= 0, cs >= 0)
                    cs = jnp.maximum(cs, 0)
                    tile = jnp.concatenate(
                        [bufs[g * 2 + c][cs // 2, 0, i, 0, cs % 2] for i in range(2)], axis=0
                    )
                    x = x + jnp.where(valid, tile.astype(F32), 0.0)
                x = x - up[g * T : g * T + T, e * T : e * T + T]
                kept = tab[U_PAT + (n + g) * 8 + j] != 0
                out[at] = jnp.where(kept, x, 0.0).astype(BF16)


def update(tab, high, low, own, buf):
    once = pl.Buffered(1)
    block = pl.BlockSpec((UM, 1024), lambda i, tab: (i, 0))
    after = pl.BlockSpec((UM, 1024), lambda i, tab: (i + 1024 // UM, 0))

    def tiles(g, c):
        def at(i, tab):
            rs = jnp.maximum(tab[U_ROW + c * 16 + i * UG + g], 0)
            return 0, rs % 2, 0, c * 4 + rs // 2, 0, 0, 0

        return pl.BlockSpec((4, 1, 2, 1, 2, 64, T), at)

    whole = pl.BlockSpec((1024, 1024), lambda i, tab: (0, 0), pipeline_mode=once)
    return pl.pallas_call(
        update_kernel,
        out_shape=jax.ShapeDtypeStruct((2048, 1024), BF16),
        grid_spec=pltpu.PrefetchScalarGridSpec(
            num_scalar_prefetch=1,
            grid=(2048 // UM,),
            in_specs=[whole, whole, after, after, block]
            + [tiles(g, c) for g in range(UG) for c in range(2)],
            out_specs=block,
        ),
        compiler_params=pltpu.CompilerParams(vmem_limit_bytes=VMEM),
        cost_estimate=pl.CostEstimate(
            flops=13 * 10**9, bytes_accessed=36 * MIB, transcendentals=0
        ),
        name="update",
    )(tab, high, low, high, low, own, *([buf] * (2 * UG)))


def shift(x, axis, k):
    return lax.ppermute(x, axis, [(i, (i + k) % 4) for i in range(4)])


def swap(x):
    return lax.ppermute(x, "core", [(0, 1), (1, 0)])


def pick(x, n):
    return lax.dynamic_index_in_dim(x, n, 0, keepdims=False)


def select(n, *cases):
    return lax.select_n(n, *cases)


def body(children, child_maps, pattern, own_cols):
    z, core, y, x = (lax.axis_index(a) for a in ALL)
    row, col = z * 2 + core, y * 4 + x
    child = row // 4

    groups = child_maps.reshape(8, 16)
    home = groups // 16
    earlier = jnp.arange(16)[None, :] < jnp.arange(16)[:, None]
    rank = jnp.sum(((home[:, :, None] == home[:, None, :]) & earlier[None]).astype(I32), axis=2)
    slot = home * 2 + rank
    orders = jnp.sum(
        jnp.where(
            slot[:, None, :] == jnp.arange(16)[None, :, None], jnp.arange(16)[None, None, :], 0
        ),
        axis=2,
    )
    order = pick(orders, row)
    column_orders = pick(orders.reshape(2, 4, 16).transpose(1, 0, 2), y)
    columns = child_maps.reshape(2, 16, 4)
    mine_columns = pick(pick(columns, child), col)
    strip_at = jnp.sum(jnp.where(mine_columns < 8, jnp.arange(4), 0))

    mine = lax.dynamic_slice(children, (0, strip_at * T), (2048, T)).reshape(16, T, T)[order]
    from_x = column_orders[:, :2] // 4

    strip = lax.all_to_all(mine.reshape(32, 64, T), ROW + ("x",), 0, 0, tiled=True)
    packed = pack_rows(children, order.astype(I32))
    own_piece = lax.dynamic_slice(own_cols, (0, col * 64), (1024, 64))
    own_piece = own_piece.reshape(8, T, 64).transpose(1, 0, 2).reshape(T, 4, T)
    first = jnp.concatenate(
        [mine[:2].transpose(1, 0, 2), own_piece, jnp.zeros((T, 2, T), BF16)], axis=1
    )
    by_half = mine.reshape(4, 2, 2, T, T)
    along_x = [
        lax.dynamic_index_in_dim(by_half, (x + k) % 4 // 2, 1, keepdims=False) for k in range(4)
    ]
    halved = pick(own_cols.reshape(2, 4, 2, T, 1024), x % 2)
    kept = lax.dynamic_index_in_dim(halved, core, 1, keepdims=False)
    given = lax.dynamic_index_in_dim(halved, 1 - core, 1, keepdims=False)
    place = lambda z, c, y, x: ((z * 2 + c) * 4 + y) * 4 + x
    chips = [(y, x) for y in range(4) for x in range(4)]
    along_x, given, first, strip = lax.optimization_barrier((along_x, given, first, strip))
    strip = jnp.take_along_axis(
        strip.reshape(2, 4, 4, 64, T), from_x[:, None, :, None, None], axis=2
    )
    buf_r = lax.all_gather(strip, COL, axis=0, tiled=False).reshape(256, 64, T)
    first = lax.all_to_all(first, ALL, 0, 0, tiled=True)
    along_x = [along_x[0]] + [shift(along_x[k], "x", k) for k in range(1, 4)]
    given = lax.ppermute(
        given, ALL, [(place(b, a // 2, b, a), place(b, 1 - a // 2, b, a)) for b, a in chips]
    )
    steps = (x - pick(from_x, child)) % 4
    slots = jnp.stack([select(steps[s], *along_x) for s in range(2)])
    along_y = [
        lax.dynamic_index_in_dim(slots, (y + k) % 4, 1, keepdims=False) for k in range(4)
    ]
    along_y = [along_y[0]] + [shift(along_y[k], "y", k) for k in range(1, 4)]
    kept = jnp.where(core == x // 2, kept, given)
    along_z = [pick(kept, (z + k) % 4) for k in range(4)]
    for k in range(1, 4):
        along_z[k] = lax.ppermute(
            along_z[k],
            ALL,
            [(place(b, c, b, a), place((b + k) % 4, c, b, a)) for b, a in chips for c in range(2)],
        )

    lead_row = jnp.sum(
        jnp.where(slot[:, None, :] == jnp.arange(2)[None, :, None], groups[:, None, :] + 1, 0), axis=2
    ) - 1
    lead_row = jnp.where(lead_row < 8, lead_row, -1)
    lead_col = jnp.sum(jnp.where(columns < 8, columns + 1, 0), axis=2) - 1
    lead_col = jnp.repeat(lead_col, 4, axis=0)
    tile = jnp.where(
        (lead_row[:, None, :] >= 0) & (lead_col[:, :, None] >= 0),
        lead_row[:, None, :] * 8 + lead_col[:, :, None],
        -1,
    ).reshape(256)
    wanted = jnp.array([i * 8 + j for i, j in LOWER])
    spread = (tile[None, :] == wanted[:, None]).astype(BF16)
    lead = nn(spread, first[:, :2].reshape(256, T))
    lead_own = first[:16, 2:6].reshape(16, 8, 64).transpose(1, 0, 2).reshape(64, T)
    lead_own = jnp.concatenate([lead_own[8 * i : 8 * i + i + 1] for i in range(8)], axis=0)
    lead = jnp.broadcast_to((lead + lead_own.astype(F32))[None], (16, 36, T))

    lead = lax.all_to_all(lead, COL, 0, 0, tiled=True)
    lead, packed = lax.optimization_barrier((lead, packed))
    here = lax.all_to_all(packed, ROW + ("x",), 0, 0, tiled=True).reshape(128, 64, T)
    by_shift = [lead] + [shift(lead, "z", k) for k in range(1, 4)]
    by_shift, along_y, along_z = lax.optimization_barrier((by_shift, along_y, along_z))
    own_q = jnp.where(z == y, along_z[0], 0) + along_z[1] + along_z[2] + along_z[3]
    own_q = own_q.reshape(2, 64, 8, T).transpose(2, 0, 1, 3).reshape(16, 64, T)
    parts = jnp.concatenate([jnp.stack(along_y).reshape(32, 64, T), own_q], axis=0)
    buf_q = lax.all_gather(parts, ROW, axis=0, tiled=False)
    lead = jnp.stack([select((z - n) % 4, *by_shift) for n in range(4)])
    other = swap(lead)
    lead = jnp.where(
        core == 0, jnp.stack([lead, other], axis=1), jnp.stack([other, lead], axis=1)
    ).reshape(128, 36, T).transpose(1, 0, 2)

    i1, i1h, i1l = panel_call(
        panel1_kernel, "panel1", 10, (F32, BF16, BF16), [(PW, PW), (T, T)], lead
    )
    i1, here = lax.optimization_barrier((i1, here))
    packed = pack_columns(here, column_orders.astype(I32).reshape(-1))
    tiles = lax.all_to_all(packed, COL, 0, 0, tiled=True).reshape(4, 2, 2, 8, 2, 64, T)
    i1, packed = lax.optimization_barrier((i1, packed))
    lh, ll, i2h, i2l = panel_call(
        panel2_kernel,
        "panel2",
        36,
        (BF16,) * 4,
        [(PW, PW), (PW, PW), (T, T), (PW, PW)],
        lead,
        i1,
    )

    by_child = groups.reshape(2, 64)
    ranks = rank.reshape(2, 4, 16)
    group = jnp.arange(4)[None, :, None]

    def find(first, count, values):
        hit = by_child[:, None, :] == (first + jnp.arange(count))[None, :, None]
        return jnp.sum(jnp.where(hit, values.reshape(2, 1, 64) + 1, 0), axis=2) - 1

    row_source = find(row * 16, 16, group * 2 + ranks).reshape(-1)
    col_source = find(col * 8, 8, group * 2 + ranks).reshape(-1)
    row_group = jnp.arange(8).reshape(2, 4, 1)
    q_rows = find(col * 8, 8, row_group * 32 + ranks * 2)
    r_rows = find(row * 16, 16, ranks * 32 + row_group * 2)
    q_cols = find(0, 8, (y - group) % 4 * 8 + ranks * 4)
    r_cols = find(0, 8, group * 64 + ranks)
    pat_rows = lax.dynamic_slice(pattern, (row * 16, 0), (16, 128))
    factor_tab = jnp.concatenate(
        [
            q_rows.T.reshape(-1),
            r_rows.T.reshape(-1),
            q_cols.reshape(-1),
            r_cols.reshape(-1),
            lax.dynamic_slice(pattern, (col * 8, 0), (8, 8)).reshape(-1),
            pat_rows[:, :8].reshape(-1),
            col * 8 + jnp.arange(8),
            row * 16 + jnp.arange(16),
            jnp.stack([8 + col]),
        ]
    ).astype(I32)
    update_tab = jnp.concatenate(
        [
            row_source,
            col_source,
            lax.dynamic_slice(pat_rows, (0, col * 8), (16, 8)).reshape(-1),
            jnp.stack([col]),
        ]
    ).astype(I32)
    high, low, fac = factor_rows(
        factor_tab, own_cols, buf_q, buf_r, (i1h, i1l, lh, ll, i2h, i2l)
    )
    return update(update_tab, high, low, own_cols, tiles), fac


def solution(mesh):
    grid = Mesh(mesh.devices.reshape(4, 2, 4, 4), ALL)
    return jax.shard_map(
        body,
        mesh=grid,
        in_specs=(P(ROW, COL), P(), P(), P(ROW, None)),
        out_specs=(P(ROW, COL), P(ALL, None)),
        check_vma=False,
    )
```

```python
import jax
import jax.numpy as jnp
from jax import lax
from jax.experimental import pallas as pl
from jax.experimental.pallas import tpu as pltpu
from jax.sharding import Mesh, PartitionSpec as P

F32 = jnp.float32
BF16 = jnp.bfloat16
I32 = jnp.int32
T = 128
PW = 512
ROW = ("z", "core")
COL = ("y", "x")
ALL = ROW + COL
FIRST = [(i, j) for i in range(4) for j in range(i + 1)]
LOWER = FIRST + [(i, j) for i in range(4, 8) for j in range(i + 1)]
HI = lax.Precision.HIGHEST
MIB = 2**20
VMEM = 56 * MIB


def nt(a, b, precision=None):
    return lax.dot_general(
        a, b, (((1,), (1,)), ((), ())), precision=precision, preferred_element_type=F32
    )


def nn(a, b, precision=None):
    return lax.dot_general(
        a, b, (((1,), (0,)), ((), ())), precision=precision, preferred_element_type=F32
    )


def halves(x):
    high = x.astype(BF16)
    return high, (x - high.astype(F32)).astype(BF16)


def nt3(a_high, a_low, b_high, b_low):
    return nt(a_high, b_high) + (nt(a_high, b_low) + nt(a_low, b_high))


def lanes(x, j):
    return jnp.broadcast_to(x[:, j : j + 1], x.shape)


def subs(x, i):
    return jnp.broadcast_to(x[i : i + 1, :], x.shape)


def rsqrt(d):
    return lax.rsqrt(d)


def invert_block(load, store):
    rest = [load(s) for s in range(16)]
    sub = lax.broadcasted_iota(I32, (8, T), 0)
    lane = lax.broadcasted_iota(I32, (8, T), 1)
    right = [(lane == sub + 8 * s).astype(F32) for s in range(16)]
    for s in range(16):
        col = [lanes(rest[s], 8 * s + t) for t in range(8)]
        a = {(i, t): subs(col[t], i) for t in range(8) for i in range(t, 8)}
        rs = []
        for t in range(8):
            rs.append(rsqrt(a[t, t]))
            for i in range(t + 1, 8):
                a[i, t] = a[i, t] * rs[t]
            for m in range(t + 1, 8):
                for i in range(m, 8):
                    a[i, m] = a[i, m] - a[i, t] * a[m, t]
        u, w = [], []
        for t in range(8):
            x, y = subs(rest[s], t), subs(right[s], t)
            for m in range(t):
                x = x - a[t, m] * u[m]
                y = y - a[t, m] * w[m]
            u.append(x * rs[t])
            w.append(y * rs[t])
        out = w[0]
        for t in range(1, 8):
            out = jnp.where(sub == t, w[t], out)
        store(s, out)
        for n in range(s + 1, 16):
            c = []
            for t in range(8):
                x = lanes(rest[n], 8 * s + t)
                for m in range(t):
                    x = x - a[t, m] * c[m]
                c.append(x * rs[t])
            x, y = rest[n], right[n]
            for t in range(8):
                x = x - c[t] * u[t]
                y = y - c[t] * w[t]
            rest[n], right[n] = x, y


def factor_panel(a, inv, out):
    out[...] = jnp.zeros((PW, PW), F32)

    def step(k, _):
        kk = pl.multiple_of(k * T, T)

        def load(s):
            return a[pl.ds(kk + 8 * s, 8), pl.ds(kk, T)]

        def store(s, v):
            inv[8 * s : 8 * s + 8, :] = v

        invert_block(load, store)
        for b in range(4):

            @pl.when(k == b)
            def _():
                lo, top = T * b, T * (b + 1)
                v = inv[...]
                if b:
                    out[lo:top, :lo] = nn(v, out[lo:top, :lo], HI)
                out[lo:top, lo:top] = v
                if b < 3:
                    col = nt(a[top:, lo:top], v, HI)
                    for j in range(b + 1, 4):
                        r = T * j
                        a[r:, r : r + T] -= nt(col[r - top :], col[r - top : r - top + T], HI)
                    out[top:, :top] -= nn(col, out[lo:top, :top], HI)

        return 0

    lax.fori_loop(0, 4, step, 0)


def panel1_kernel(lead_ref, i1_ref, i1h, i1l, a, inv):
    for n, (i, j) in enumerate(FIRST):
        a[i * T : i * T + T, j * T : j * T + T] = lead_ref[n]
    factor_panel(a, inv, i1_ref)
    i1h[...], i1l[...] = halves(i1_ref[...].T)


def panel2_kernel(lead_ref, i1_ref, lh, ll, i2h, i2l, a, low, inv, i2):
    for n, (i, j) in enumerate(LOWER):
        if i < 4:
            continue
        if j < 4:
            low[i * T - PW : i * T - PW + T, j * T : j * T + T] = lead_ref[n]
        else:
            a[i * T - PW : i * T - PW + T, j * T - PW : j * T - PW + T] = lead_ref[n]
    col = nt(low[...], i1_ref[...], HI)
    lh[...], ll[...] = halves(col.T)
    for j in range(4):
        r = T * j
        a[r:, r : r + T] -= nt(col[r:], col[r : r + T], HI)
    factor_panel(a, inv, i2)
    i2h[...], i2l[...] = halves(i2[...].T)


def panel_call(kernel, name, tiles, outs, scratch, lead, *args):
    whole = pl.BlockSpec((PW, PW), lambda i: (0, 0), pipeline_mode=pl.Buffered(1))
    return pl.pallas_call(
        kernel,
        out_shape=tuple(jax.ShapeDtypeStruct((PW, PW), t) for t in outs),
        grid=(1,),
        in_specs=[pl.BlockSpec((tiles, T, T), lambda i: (0, 0, 0), pipeline_mode=pl.Buffered(1))]
        + [whole] * len(args),
        out_specs=[whole] * len(outs),
        scratch_shapes=[pltpu.VMEM(x, F32) for x in scratch],
        compiler_params=pltpu.CompilerParams(vmem_limit_bytes=24 * MIB),
        cost_estimate=pl.CostEstimate(flops=25 * 10**9, bytes_accessed=4 * MIB, transcendentals=0),
        name=name,
    )(lead, *args)


def pack_rows_kernel(tab, top, low, out):
    for t, ref in enumerate((top, low)):
        for h in range(2):
            for k in range(4):
                out[t * 2 + h, k] = ref[64 * h : 64 * h + 64, k * T : k * T + T]


def pack_rows(children, order):
    return pl.pallas_call(
        pack_rows_kernel,
        out_shape=jax.ShapeDtypeStruct((32, 4, 64, T), BF16),
        grid_spec=pltpu.PrefetchScalarGridSpec(
            num_scalar_prefetch=1,
            grid=(8,),
            in_specs=[
                pl.BlockSpec((T, PW), lambda p, tab: (tab[2 * p], 0)),
                pl.BlockSpec((T, PW), lambda p, tab: (tab[2 * p + 1], 0)),
            ],
            out_specs=pl.BlockSpec((4, 4, 64, T), lambda p, tab: (p, 0, 0, 0)),
        ),
        compiler_params=pltpu.CompilerParams(vmem_limit_bytes=16 * MIB),
        cost_estimate=pl.CostEstimate(flops=0, bytes_accessed=4 * MIB, transcendentals=0),
        name="pack_rows",
    )(order, children, children)


def pack_columns_kernel(tab, ref, out):
    p = pl.program_id(0)
    for g in range(8):
        for s in range(2):
            part = ref[g * 16 + tab[g // 4 * 16 + p * 2 + s]]
            for q in range(2):
                out[q, g, s] = part


def pack_columns(halves_here, orders):
    return pl.pallas_call(
        pack_columns_kernel,
        out_shape=jax.ShapeDtypeStruct((16, 8, 2, 64, T), BF16),
        grid_spec=pltpu.PrefetchScalarGridSpec(
            num_scalar_prefetch=1,
            grid=(8,),
            in_specs=[
                pl.BlockSpec((128, 64, T), lambda p, tab: (0, 0, 0), pipeline_mode=pl.Buffered(1))
            ],
            out_specs=pl.BlockSpec((2, 8, 2, 64, T), lambda p, tab: (p, 0, 0, 0, 0)),
        ),
        compiler_params=pltpu.CompilerParams(vmem_limit_bytes=16 * MIB),
        cost_estimate=pl.CostEstimate(flops=0, bytes_accessed=6 * MIB, transcendentals=0),
        name="pack_columns",
    )(orders, halves_here)


TM = 512
SUB = 128
QS = 1024 // TM
RS = 2048 // TM
G = TM // T
STEPS = QS + RS
F_ROW, F_COL, F_PAT, F_AT, F_SHARE = 0, 48, 80, 272, 296


def nn3(a_high, a_low, b_high, b_low):
    return nn(jnp.concatenate([a_high, a_high, a_low], axis=1), jnp.concatenate([b_high, b_low, b_high], axis=0))


def factor_kernel(
    tab, own_q, own_r, buf_q, buf_r, i1h, i1l, lh, ll, i2h, i2l, high, low, fac, sh, sl, rest, tiles, sem
):
    step = pl.program_id(0)

    def load(n):
        ref = (buf_q.at[:, pl.ds(0, 32)], buf_r)[n]
        return pltpu.make_async_copy(ref, tiles.at[pl.ds(8 * n, 8)], sem.at[n])

    def assemble(i, slot, g):
        side = (i >= QS).astype(I32)
        stride = jnp.where(side == 1, 16, 1)
        n = i * G + g
        for j in range(8):
            kept = tab[F_PAT + n * 8 + j] != 0
            at = [(tab[F_ROW + n * 2 + c], tab[F_COL + side * 16 + c * 8 + j]) for c in range(2)]
            valid = [jnp.logical_and(a >= 0, b >= 0) for a, b in at]
            at = [side * 256 + a + b for a, b in at]
            for h in range(2):
                line = slice(g * T + 64 * h, g * T + 64 * h + 64)
                x = jnp.where(side == 1, own_r[line, j * T : j * T + T], own_q[g, j * 2 + h])
                x = jnp.where(kept, x, jnp.zeros_like(x)).astype(F32)
                for c in range(2):
                    half = jnp.where(valid[c], at[c] + h * stride, 512)
                    x = x + tiles[half // 32, half % 32].astype(F32)
                if j < 4:
                    place = slice(j * T, j * T + T)
                    sh[slot, line, place], sl[slot, line, place] = halves(x)
                else:
                    rest[slot, line, j * T - PW : j * T - PW + T] = x

    def by_inverse(xh, xl, ih, il):
        left = nn3(xh[:, :256], xl[:, :256], ih[:256, :256], il[:256, :256])
        right = nn3(xh, xl, ih[:, 256:], il[:, 256:])
        return jnp.concatenate([left, right], axis=1)

    def multiply(i, slot, between):
        count, lines = TM // SUB, SUB // T
        zero = jnp.zeros((T, PW), BF16)
        at = [slice(c * SUB, c * SUB + SUB) for c in range(count)]
        f0 = [by_inverse(sh[slot, x], sl[slot, x], i1h, i1l) for x in at]
        between(0)
        ups, f1 = [], []
        for c in range(count):
            f0h, f0l = halves(f0[c])
            ups.append(nn3(f0h, f0l, lh[...], ll[...]))
            for g in range(lines):
                first = tab[F_AT + i * G + c * lines + g]
                line, to = slice(g * T, g * T + T), slice(c * SUB + g * T, c * SUB + g * T + T)
                high[to, :PW] = jnp.where(first >= 4, f0h[line], zero)
                low[to, :PW] = jnp.where(first >= 4, f0l[line], zero)
        between(1)
        for c in range(count):
            rows = []
            for g in range(lines):
                n = i * G + c * lines + g
                line = slice(g * T, g * T + T)
                row = []
                for j in range(4):
                    keep = jnp.logical_and(tab[F_PAT + n * 8 + 4 + j] != 0, tab[F_AT + n] >= 4)
                    part = ups[c][line, j * T : j * T + T]
                    old = rest[slot, c * SUB + g * T : c * SUB + g * T + T, j * T : j * T + T]
                    row.append(old - jnp.where(keep, part, 0.0))
                rows.append(jnp.concatenate(row, axis=1))
            f1.append(by_inverse(*halves(jnp.concatenate(rows, axis=0)), i2h, i2l))
        between(2)
        for c in range(count):
            f1h, f1l = halves(f1[c])
            for g in range(lines):
                first = tab[F_AT + i * G + c * lines + g]
                line, to = slice(g * T, g * T + T), slice(c * SUB + g * T, c * SUB + g * T + T)
                high[to, PW:] = jnp.where(first >= 8, f1h[line], zero)
                low[to, PW:] = jnp.where(first >= 8, f1l[line], zero)
        return list(zip(f0, f1))

    @pl.when(step == 0)
    def _():
        load(0).start()
        load(1).start()
        tiles[16, 0] = jnp.zeros((64, T), BF16)
        load(0).wait()
        load(1).wait()
        for g in range(G):
            assemble(step, 0, g)

    @pl.when(step > 0)
    def _():
        slot = step % 2
        nxt = jnp.minimum(step, STEPS - 1)

        def between(k):
            for g in range(G):
                if g * 3 // G == k:
                    assemble(nxt, slot, g)

        keep = multiply(step - 1, 1 - slot, between)
        for g in range(G):
            c, e = divmod(g, SUB // T)

            @pl.when(tab[F_SHARE] == (step - 1) * G + g)
            def _():
                f0, f1 = keep[c]
                fac[:, :PW] = f0[e * T : e * T + T]
                fac[:, PW:] = jnp.where(tab[F_AT + (step - 1) * G + g] >= 4, f1[e * T : e * T + T], 0.0)


def factor_rows(tab, own_r, buf_q, buf_r, inverses):
    small = pl.BlockSpec((PW, PW), lambda i, tab: (0, 0), pipeline_mode=pl.Buffered(1))
    out = pl.BlockSpec((TM, 1024), lambda i, tab: (jnp.maximum(i - 1, 0), 0))
    shape = jax.ShapeDtypeStruct((3072, 1024), BF16)
    return pl.pallas_call(
        factor_kernel,
        out_shape=(shape, shape, jax.ShapeDtypeStruct((T, 1024), F32)),
        grid_spec=pltpu.PrefetchScalarGridSpec(
            num_scalar_prefetch=1,
            grid=(STEPS + 1,),
            in_specs=[
                pl.BlockSpec((G, 16, 64, T), lambda i, tab: (jnp.minimum(i, QS - 1), 2, 0, 0)),
                pl.BlockSpec((TM, 1024), lambda i, tab: (jnp.clip(i - QS, 0, RS - 1), 0)),
                pl.BlockSpec(memory_space=pl.ANY),
                pl.BlockSpec(memory_space=pl.ANY),
            ]
            + [small] * 6,
            out_specs=[out, out, pl.BlockSpec((T, 1024), lambda i, tab: (0, 0))],
            scratch_shapes=[
                pltpu.VMEM((2, TM, PW), BF16),
                pltpu.VMEM((2, TM, PW), BF16),
                pltpu.VMEM((2, TM, PW), F32),
                pltpu.VMEM((17, 32, 64, T), BF16),
                pltpu.SemaphoreType.DMA((2,)),
            ],
        ),
        compiler_params=pltpu.CompilerParams(vmem_limit_bytes=VMEM),
        cost_estimate=pl.CostEstimate(
            flops=16 * 10**9, bytes_accessed=30 * MIB, transcendentals=0
        ),
        name="factor_rows",
    )(tab, buf_q, own_r, buf_q, buf_r.reshape(8, 32, 64, T), *inverses)


UM = 256
UG = UM // T
U_ROW, U_COL, U_PAT, U_LEFT = 0, 32, 48, 176


def update_kernel(tab, qh, ql, rh, rl, own, *rest):
    bufs, out = rest[: 2 * UG], rest[2 * UG]
    n = pl.program_id(0) * UG
    at_left = tab[U_LEFT] == 0
    fh, fl = rh[...], rl[...]
    f3 = jnp.concatenate([fh, fh, fl], axis=1)
    for h in range(4):
        qr = slice(h * 256, h * 256 + 256)
        up = nt(f3, jnp.concatenate([qh[qr, :], ql[qr, :], qh[qr, :]], axis=1))
        for g in range(UG):
            for e in range(2):
                j = h * 2 + e
                at = slice(g * T, g * T + T), slice(j * T, j * T + T)
                x = jnp.where(at_left, own[at].astype(F32), 0.0)
                for c in range(2):
                    cs = tab[U_COL + c * 8 + j]
                    valid = jnp.logical_and(tab[U_ROW + c * 16 + n + g] >= 0, cs >= 0)
                    cs = jnp.maximum(cs, 0)
                    tile = jnp.concatenate(
                        [bufs[g * 2 + c][cs // 2, 0, i, 0, cs % 2] for i in range(2)], axis=0
                    )
                    x = x + jnp.where(valid, tile.astype(F32), 0.0)
                x = x - up[g * T : g * T + T, e * T : e * T + T]
                kept = tab[U_PAT + (n + g) * 8 + j] != 0
                out[at] = jnp.where(kept, x, 0.0).astype(BF16)


def update(tab, high, low, own, buf):
    once = pl.Buffered(1)
    block = pl.BlockSpec((UM, 1024), lambda i, tab: (i, 0))
    after = pl.BlockSpec((UM, 1024), lambda i, tab: (i + 1024 // UM, 0))

    def tiles(g, c):
        def at(i, tab):
            rs = jnp.maximum(tab[U_ROW + c * 16 + i * UG + g], 0)
            return 0, rs % 2, 0, c * 4 + rs // 2, 0, 0, 0

        return pl.BlockSpec((4, 1, 2, 1, 2, 64, T), at)

    whole = pl.BlockSpec((1024, 1024), lambda i, tab: (0, 0), pipeline_mode=once)
    return pl.pallas_call(
        update_kernel,
        out_shape=jax.ShapeDtypeStruct((2048, 1024), BF16),
        grid_spec=pltpu.PrefetchScalarGridSpec(
            num_scalar_prefetch=1,
            grid=(2048 // UM,),
            in_specs=[whole, whole, after, after, block]
            + [tiles(g, c) for g in range(UG) for c in range(2)],
            out_specs=block,
        ),
        compiler_params=pltpu.CompilerParams(vmem_limit_bytes=VMEM),
        cost_estimate=pl.CostEstimate(
            flops=13 * 10**9, bytes_accessed=36 * MIB, transcendentals=0
        ),
        name="update",
    )(tab, high, low, high, low, own, *([buf] * (2 * UG)))


def shift(x, axis, k):
    return lax.ppermute(x, axis, [(i, (i + k) % 4) for i in range(4)])


def swap(x):
    return lax.ppermute(x, "core", [(0, 1), (1, 0)])


def pick(x, n):
    return lax.dynamic_index_in_dim(x, n, 0, keepdims=False)


def select(n, *cases):
    return lax.select_n(n, *cases)


def body(children, child_maps, pattern, own_cols):
    z, core, y, x = (lax.axis_index(a) for a in ALL)
    row, col = z * 2 + core, y * 4 + x
    child = row // 4

    groups = child_maps.reshape(8, 16)
    home = groups // 16
    earlier = jnp.arange(16)[None, :] < jnp.arange(16)[:, None]
    rank = jnp.sum(((home[:, :, None] == home[:, None, :]) & earlier[None]).astype(I32), axis=2)
    slot = home * 2 + rank
    orders = jnp.sum(
        jnp.where(
            slot[:, None, :] == jnp.arange(16)[None, :, None], jnp.arange(16)[None, None, :], 0
        ),
        axis=2,
    )
    order = pick(orders, row)
    column_orders = pick(orders.reshape(2, 4, 16).transpose(1, 0, 2), y)
    columns = child_maps.reshape(2, 16, 4)
    mine_columns = pick(pick(columns, child), col)
    strip_at = jnp.sum(jnp.where(mine_columns < 8, jnp.arange(4), 0))

    mine = lax.dynamic_slice(children, (0, strip_at * T), (2048, T)).reshape(16, T, T)[order]
    from_x = column_orders[:, :2] // 4

    strip = lax.all_to_all(mine.reshape(32, 64, T), ROW + ("x",), 0, 0, tiled=True)
    packed = pack_rows(children, order.astype(I32))
    own_piece = lax.dynamic_slice(own_cols, (0, col * 64), (1024, 64))
    own_piece = own_piece.reshape(8, T, 64).transpose(1, 0, 2).reshape(T, 4, T)
    first = jnp.concatenate(
        [mine[:2].transpose(1, 0, 2), own_piece, jnp.zeros((T, 2, T), BF16)], axis=1
    )
    by_half = mine.reshape(4, 2, 2, T, T)
    along_x = [
        lax.dynamic_index_in_dim(by_half, (x + k) % 4 // 2, 1, keepdims=False) for k in range(4)
    ]
    halved = pick(own_cols.reshape(2, 4, 2, T, 1024), x % 2)
    kept = lax.dynamic_index_in_dim(halved, core, 1, keepdims=False)
    given = lax.dynamic_index_in_dim(halved, 1 - core, 1, keepdims=False)
    place = lambda z, c, y, x: ((z * 2 + c) * 4 + y) * 4 + x
    chips = [(y, x) for y in range(4) for x in range(4)]
    along_x, given, first, strip = lax.optimization_barrier((along_x, given, first, strip))
    strip = jnp.take_along_axis(
        strip.reshape(2, 4, 4, 64, T), from_x[:, None, :, None, None], axis=2
    )
    buf_r = lax.all_gather(strip, COL, axis=0, tiled=False).reshape(256, 64, T)
    first = lax.all_to_all(first, ALL, 0, 0, tiled=True)
    along_x = [along_x[0]] + [shift(along_x[k], "x", k) for k in range(1, 4)]
    given = lax.ppermute(
        given, ALL, [(place(b, a // 2, b, a), place(b, 1 - a // 2, b, a)) for b, a in chips]
    )
    steps = (x - pick(from_x, child)) % 4
    slots = jnp.stack([select(steps[s], *along_x) for s in range(2)])
    along_y = [
        lax.dynamic_index_in_dim(slots, (y + k) % 4, 1, keepdims=False) for k in range(4)
    ]
    along_y = [along_y[0]] + [shift(along_y[k], "y", k) for k in range(1, 4)]
    kept = jnp.where(core == x // 2, kept, given)
    along_z = [pick(kept, (z + k) % 4) for k in range(4)]
    for k in range(1, 4):
        along_z[k] = lax.ppermute(
            along_z[k],
            ALL,
            [(place(b, c, b, a), place((b + k) % 4, c, b, a)) for b, a in chips for c in range(2)],
        )

    lead_row = jnp.sum(
        jnp.where(slot[:, None, :] == jnp.arange(2)[None, :, None], groups[:, None, :] + 1, 0), axis=2
    ) - 1
    lead_row = jnp.where(lead_row < 8, lead_row, -1)
    lead_col = jnp.sum(jnp.where(columns < 8, columns + 1, 0), axis=2) - 1
    lead_col = jnp.repeat(lead_col, 4, axis=0)
    tile = jnp.where(
        (lead_row[:, None, :] >= 0) & (lead_col[:, :, None] >= 0),
        lead_row[:, None, :] * 8 + lead_col[:, :, None],
        -1,
    ).reshape(256)
    wanted = jnp.array([i * 8 + j for i, j in LOWER])
    spread = (tile[None, :] == wanted[:, None]).astype(BF16)
    lead = nn(spread, first[:, :2].reshape(256, T))
    lead_own = first[:16, 2:6].reshape(16, 8, 64).transpose(1, 0, 2).reshape(64, T)
    lead_own = jnp.concatenate([lead_own[8 * i : 8 * i + i + 1] for i in range(8)], axis=0)
    lead = jnp.broadcast_to((lead + lead_own.astype(F32))[None], (16, 36, T))

    lead = lax.all_to_all(lead, COL, 0, 0, tiled=True)
    by_shift = [lead] + [shift(lead, "z", k) for k in range(1, 4)]
    by_shift, along_y, along_z, packed = lax.optimization_barrier(
        (by_shift, along_y, along_z, packed)
    )
    here = lax.all_to_all(packed, ROW + ("x",), 0, 0, tiled=True).reshape(128, 64, T)
    own_q = jnp.where(z == y, along_z[0], 0) + along_z[1] + along_z[2] + along_z[3]
    own_q = own_q.reshape(2, 64, 8, T).transpose(2, 0, 1, 3).reshape(16, 64, T)
    parts = jnp.concatenate([jnp.stack(along_y).reshape(32, 64, T), own_q], axis=0)
    buf_q = lax.all_gather(parts, ROW, axis=0, tiled=False)
    lead = jnp.stack([select((z - n) % 4, *by_shift) for n in range(4)])
    other = swap(lead)
    lead = jnp.where(
        core == 0, jnp.stack([lead, other], axis=1), jnp.stack([other, lead], axis=1)
    ).reshape(128, 36, T).transpose(1, 0, 2)

    i1, i1h, i1l = panel_call(
        panel1_kernel, "panel1", 10, (F32, BF16, BF16), [(PW, PW), (T, T)], lead
    )
    i1, here = lax.optimization_barrier((i1, here))
    packed = pack_columns(here, column_orders.astype(I32).reshape(-1))
    tiles = lax.all_to_all(packed, COL, 0, 0, tiled=True).reshape(4, 2, 2, 8, 2, 64, T)
    i1, packed = lax.optimization_barrier((i1, packed))
    lh, ll, i2h, i2l = panel_call(
        panel2_kernel,
        "panel2",
        36,
        (BF16,) * 4,
        [(PW, PW), (PW, PW), (T, T), (PW, PW)],
        lead,
        i1,
    )

    by_child = groups.reshape(2, 64)
    ranks = rank.reshape(2, 4, 16)
    group = jnp.arange(4)[None, :, None]

    def find(first, count, values):
        hit = by_child[:, None, :] == (first + jnp.arange(count))[None, :, None]
        return jnp.sum(jnp.where(hit, values.reshape(2, 1, 64) + 1, 0), axis=2) - 1

    row_source = find(row * 16, 16, group * 2 + ranks).reshape(-1)
    col_source = find(col * 8, 8, group * 2 + ranks).reshape(-1)
    row_group = jnp.arange(8).reshape(2, 4, 1)
    q_rows = find(col * 8, 8, row_group * 32 + ranks * 2)
    r_rows = find(row * 16, 16, ranks * 32 + row_group * 2)
    q_cols = find(0, 8, (y - group) % 4 * 8 + ranks * 4)
    r_cols = find(0, 8, group * 64 + ranks)
    pat_rows = lax.dynamic_slice(pattern, (row * 16, 0), (16, 128))
    factor_tab = jnp.concatenate(
        [
            q_rows.T.reshape(-1),
            r_rows.T.reshape(-1),
            q_cols.reshape(-1),
            r_cols.reshape(-1),
            lax.dynamic_slice(pattern, (col * 8, 0), (8, 8)).reshape(-1),
            pat_rows[:, :8].reshape(-1),
            col * 8 + jnp.arange(8),
            row * 16 + jnp.arange(16),
            jnp.stack([8 + col]),
        ]
    ).astype(I32)
    update_tab = jnp.concatenate(
        [
            row_source,
            col_source,
            lax.dynamic_slice(pat_rows, (0, col * 8), (16, 8)).reshape(-1),
            jnp.stack([col]),
        ]
    ).astype(I32)
    high, low, fac = factor_rows(
        factor_tab, own_cols, buf_q, buf_r, (i1h, i1l, lh, ll, i2h, i2l)
    )
    return update(update_tab, high, low, own_cols, tiles), fac


def solution(mesh):
    grid = Mesh(mesh.devices.reshape(4, 2, 4, 4), ALL)
    return jax.shard_map(
        body,
        mesh=grid,
        in_specs=(P(ROW, COL), P(), P(), P(ROW, None)),
        out_specs=(P(ROW, COL), P(ALL, None)),
        check_vma=False,
    )
```
